128 devices in a mesh: cell: 16 (over x, y), cyc: 2 (over core), feat: 4 (over z).
Axes of the slice: x: 4, y: 4, z: 4, core: 2. Of those that a mesh axis runs over, the one named last changes fastest.
Arguments:
- tensor: float32 [2048, 512, 512], P('cell', 'cyc', 'feat'), may hold values from -750 to 750
- present: int32 [128, 32], P('cell', 'cyc'), may hold values from 0 to 1, as said below
- cyc_factor: float32 [512, 32], P('cyc'), may hold values from -6 to 6
- feat_factor: float32 [512, 32], P('feat'), may hold values from -6 to 6
Outputs:
- cell_unit: float32 [2048, 32], P('cell')
- cyc_unit: float32 [512, 32], P('cyc')
- feat_unit: float32 [512, 32], P('feat')
The draws below stay inside these ranges and needn't reach their ends.
Inputs may be any that keep to these rules, and one draw needn't show every extreme that they name: `present`: in each row the ones form a prefix of 8 or more blocks; some row is all ones, and some row has exactly 8 ones.
All inputs are finite; a program needn't handle non-finite values.
Results may differ from the reference program's by a relative error of at most 0.00017.
Values sent between devices are 32-bit elements; how exact they have to be, the bound alone decides.
No kernel may reach another device: no remote copies, remote signals or barrier semaphores. Data moves between devices by JAX's collectives and lax.ppermute only.
A program may use at most 128 MiB of HBM per device.

```python
import math
import jax
import jax.numpy as jnp
from jax import lax

FEAT = 512
RANK = 32
BLK_CELL = 16
BLK_CYC = 16
CELL = 2048
CYC = 512


def draw_tensor(key, part):
    key = jax.random.fold_in(key, 11)
    key_base, key_feat, key_cyc = jax.random.split(key, 3)
    row_scale = 10.0 ** (jnp.arange(CELL, dtype=jnp.float32) / CELL)
    feat_scale = jnp.exp(jax.random.uniform(key_feat, (FEAT,), jnp.float32, 0.0, math.log(10.0)))
    cyc_scale = jax.random.uniform(key_cyc, (CYC,), jnp.float32, 0.5, 1.5)
    base = jnp.clip(jax.random.normal(key_base, (CELL, CYC, FEAT), jnp.float32), -5.0, 5.0)
    return base * row_scale[:, None, None] * cyc_scale[None, :, None] * feat_scale[None, None, :]


def draw_present(key, part):
    key = jax.random.fold_in(key, 5)
    cell_blocks = CELL // BLK_CELL
    cyc_blocks = CYC // BLK_CYC
    key_life, key_first, key_second = jax.random.split(key, 3)
    shortest = cyc_blocks // 4
    life = jax.random.randint(key_life, (cell_blocks,), shortest, cyc_blocks + 1)
    first = jax.random.randint(key_first, (), 0, cell_blocks)
    second = (first + 1 + jax.random.randint(key_second, (), 0, cell_blocks - 1)) % cell_blocks
    life = life.at[first].set(cyc_blocks).at[second].set(shortest)
    columns = jnp.arange(cyc_blocks, dtype=jnp.int32)
    return (columns[None, :] < life[:, None]).astype(jnp.int32)


def level_of(own_key, dims, shards, least, high):
    def one(dim, parts):
        draws = jax.random.uniform(jax.random.fold_in(jax.random.fold_in(own_key, 6), dim), (parts,), jnp.float32, least / len(shards), high / len(shards))
        return jnp.repeat(jnp.exp(draws), dims[dim] // parts).reshape((-1,) + (1,) * (len(dims) - dim - 1))

    loudness = one(*shards[0])
    for cut in shards[1:]:
        loudness = loudness * one(*cut)
    return loudness


def noise(key, dims, scale, reach, pieces=(), held_as=jnp.bfloat16):
    drawn = scale * jax.random.normal(key, dims, jnp.float32)
    if pieces:
        drawn = drawn * level_of(key, dims, pieces, -0.22, 0.18)
    return jnp.clip(drawn, -reach, reach).astype(held_as)


def setup_inputs(seed: int = 0) -> dict:
    arg_keys = jax.random.split(jax.random.key(seed), 5)
    return {
        "tensor": draw_tensor(jax.random.fold_in(arg_keys[4], 71), 0),
        "present": draw_present(jax.random.fold_in(arg_keys[4], 71), 0),
        "cyc_factor": noise(arg_keys[2], (CYC, RANK), 1.0, 6.0, ((0, 2),), jnp.float32),
        "feat_factor": noise(arg_keys[3], (FEAT, RANK), 1.0, 6.0, ((0, 4),), jnp.float32),
    }


EPS = 1e-06
HIGHEST_MODE = lax.Precision.HIGHEST

def expand_mask(present):
    spread = jnp.repeat(present.astype(jnp.float32), BLK_CELL, axis=0)
    return jnp.repeat(spread, BLK_CYC, axis=1)

def local_gram(rows):
    return lax.dot_general(rows, rows, (((0,), (0,)), ((), ())), precision=HIGHEST_MODE)

def solve_rows(rhs, gram):
    factor = jnp.linalg.cholesky(gram)
    return jax.scipy.linalg.cho_solve((factor, True), rhs.T).T

def unit_columns(raw, gram, count):
    scale = jnp.sqrt(jnp.diagonal(gram) / count + EPS)
    return (raw / scale, gram / (scale[:, None] * scale[None, :]))

def reference(tensor, present, cyc_factor, feat_factor):
    recorded = expand_mask(present)
    flat = tensor.reshape(CELL * CYC, FEAT)
    gram_cyc = local_gram(cyc_factor)
    gram_feat = local_gram(feat_factor)
    contracted = jnp.dot(flat, feat_factor, precision=HIGHEST_MODE).reshape(CELL, CYC, RANK)
    contracted = contracted * recorded[:, :, None]
    part_cell = jnp.einsum('ijr,jr->ir', contracted, cyc_factor, precision=HIGHEST_MODE)
    raw_cell = solve_rows(part_cell, gram_cyc * gram_feat)
    cell_unit, unit_gram_cell = unit_columns(raw_cell, local_gram(raw_cell), float(CELL))
    part_cyc = jnp.einsum('ijr,ir->jr', contracted, cell_unit, precision=HIGHEST_MODE)
    raw_cyc = solve_rows(part_cyc, unit_gram_cell * gram_feat)
    cyc_unit, unit_gram_cyc = unit_columns(raw_cyc, local_gram(raw_cyc), float(CYC))
    joint = cell_unit[:, None, :] * cyc_unit[None, :, :] * recorded[:, :, None]
    part_feat = lax.dot_general(flat, joint.reshape(CELL * CYC, RANK), (((0,), (0,)), ((), ())), precision=HIGHEST_MODE)
    raw_feat = solve_rows(part_feat, unit_gram_cell * unit_gram_cyc)
    feat_unit, unused_gram = unit_columns(raw_feat, local_gram(raw_feat), float(FEAT))
    return (cell_unit, cyc_unit, feat_unit)
```

```python
import functools

import jax
import jax.numpy as jnp
from jax import lax
from jax.experimental import pallas as pl
from jax.experimental.pallas import tpu as pltpu
from jax.sharding import PartitionSpec as P

BLK = 16
EPS = 1e-06
HIGHEST = lax.Precision.HIGHEST
F32 = jnp.float32
BF16 = jnp.bfloat16
VMEM_LIMIT = 48 * 1024 * 1024
LANES = 128


def dot(a, b, dims, precision=None):
    return lax.dot_general(a, b, (dims, ((), ())), precision=precision, preferred_element_type=F32)


def split(x):
    hi = x.astype(BF16)
    return hi, (x - hi.astype(F32)).astype(BF16)


def lane_iota(rows, cols=LANES):
    return lax.broadcasted_iota(jnp.int32, (rows, cols), 1)


def wide_gram(rows_t):
    r, n = rows_t.shape
    padded = jnp.concatenate([rows_t, jnp.zeros((LANES - r, n), F32)], axis=0)
    return dot(rows_t, padded, ((1,), (1,)), HIGHEST)


def pack(wide):
    out = wide[0:8]
    for q in range(1, 4):
        out = out + pltpu.roll(wide[8 * q : 8 * q + 8], 32 * q, 1)
    return out


def unpack(packed):
    used = lane_iota(8) < 32
    parts = [packed if q == 0 else pltpu.roll(packed, LANES - 32 * q, 1) for q in range(4)]
    return jnp.concatenate([jnp.where(used, x, 0.0) for x in parts], axis=0)


def inverse(m):
    r = m.shape[0]
    row_id = lax.broadcasted_iota(jnp.int32, m.shape, 0)
    col_id = lax.broadcasted_iota(jnp.int32, m.shape, 1)
    for p in range(r):
        row = m[p : p + 1, :]
        col = m[:, p : p + 1]
        d = 1.0 / m[p : p + 1, p : p + 1]
        on_col = col_id == p
        row = jnp.where(on_col[0:1], d, row * d)
        m = jnp.where(row_id == p, row, jnp.where(on_col, 0.0, m) - col * row)
    return m


def scales(wide, count):
    r = wide.shape[0]
    row_id = lax.broadcasted_iota(jnp.int32, wide.shape, 0)
    col_id = lax.broadcasted_iota(jnp.int32, wide.shape, 1)
    diag = jnp.where(row_id == col_id, wide, 0.0)
    col = jnp.sqrt(jnp.sum(diag, axis=1, keepdims=True) / count + EPS)
    row = jnp.sqrt(jnp.sum(diag, axis=0, keepdims=True) / count + EPS)
    return col, row


def expand_rows(present):
    nb, mb = present.shape
    first = lax.broadcasted_iota(jnp.int32, (mb, mb * BLK), 0) * BLK
    cyc = lax.broadcasted_iota(jnp.int32, (mb, mb * BLK), 1)
    spread = jnp.where((cyc >= first) & (cyc < first + BLK), 1.0, 0.0)
    return dot(present.astype(F32), spread, ((1,), (0,)), HIGHEST)


def contract_kernel(present, cyc_t, feat_t, tensor, c_out, pay, t_buf, c_buf, mask, lhs, t_sem, c_sem):
    cells = tensor.shape[0]
    chunks = cells // BLK
    rank = cyc_t.shape[0]

    def fetch(n):
        rows = pl.ds(n * BLK, BLK)
        return pltpu.make_async_copy(tensor.at[rows], t_buf.at[rows], t_sem.at[n])

    def flush(n):
        rows = pl.ds(n * BLK, BLK)
        return pltpu.make_async_copy(c_buf.at[rows], c_out.at[rows], c_sem.at[n])

    for n in range(chunks):
        fetch(n).start()
    mask[...] = expand_rows(present[...])
    hi, lo = split(feat_t[...])
    lhs[0:rank, :] = jnp.concatenate([hi, hi], axis=1)
    lhs[rank:, :] = jnp.concatenate([lo, jnp.zeros_like(lo)], axis=1)
    gram_cyc = pack(wide_gram(cyc_t[...]))
    gram_feat = pack(wide_gram(feat_t[...]))
    lane = lane_iota(rank)

    def step(n, part):
        fetch(n).wait()
        row = mask[pl.ds(n, 1), :]
        left = lhs[...]
        for q in range(BLK):
            i = n * BLK + q
            hi, lo = split(t_buf[i])
            out = dot(left, jnp.concatenate([hi, lo], axis=1), ((1,), (1,)))
            c = out[:rank] * row + out[rank:] * row
            c_buf[i] = c
            total = jnp.sum(c * cyc_t[...], axis=1, keepdims=True)
            part = jnp.where(lane == i, total, part)
        flush(n).start()
        return part

    part = lax.fori_loop(0, chunks, step, jnp.zeros((rank, cells), F32))
    for d in range(pay.shape[0]):
        pay[d, 0:rank, :] = part
        pay[d, rank : rank + 8, :] = gram_cyc
        pay[d, rank + 8 :, :] = gram_feat
    for n in range(chunks):
        flush(n).wait()


def cells_kernel(got, c_in, raw_out, gram_feat_out, pay, c_buf, c_sem):
    cells, rank = c_in.shape[0], c_in.shape[1]
    chunks = cells // BLK

    def fetch(n):
        rows = pl.ds(n * BLK, BLK)
        return pltpu.make_async_copy(c_in.at[rows], c_buf.at[rows], c_sem.at[n])

    for n in range(chunks):
        fetch(n).start()
    part = got[0, 0:rank, :]
    for d in range(1, 8):
        part = part + got[d, 0:rank, :]
    gram_cyc = unpack(got[0, rank : rank + 8, :] + got[4, rank : rank + 8, :])
    gram_feat = got[0, rank + 8 :, :]
    for d in range(1, 4):
        gram_feat = gram_feat + got[d, rank + 8 :, :]
    gram_feat = unpack(gram_feat)
    gram_feat_out[...] = gram_feat
    inv = inverse(gram_cyc * gram_feat)
    raw = dot(inv[:, :rank], part, ((1,), (0,)), HIGHEST)
    raw_out[...] = raw
    gram = pack(wide_gram(raw))

    def step(n, carry):
        fetch(n).wait()
        total, rolled = carry
        for q in range(BLK):
            total = total + c_buf[n * BLK + q] * rolled[:, q : q + 1]
        return total, pltpu.roll(rolled, LANES - BLK, 1)

    total, _ = lax.fori_loop(0, chunks, step, (jnp.zeros((rank, c_in.shape[2]), F32), raw))
    for d in range(pay.shape[0]):
        pay[d, 0:rank, :] = total[:, :LANES]
        pay[d, rank : 2 * rank, :] = total[:, LANES:]
        pay[d, 2 * rank :, :] = gram


def spread_kernel(rows, got, pay):
    total = got[0]
    for d in range(1, got.shape[0]):
        total = total + got[d]
    for d in range(pay.shape[0]):
        pay[d, :rows, :] = total[:rows]
        pay[d, rows:, :] = got[0, rows:, :]


def cycles_kernel(
    cells_all, present, got, raw_cell, gram_feat, tensor,
    cell_unit, raw_cyc_out, unit_out, pay, t_buf, mask, raw_cyc, wide, t_sem,
):
    cells = tensor.shape[0]
    chunks = cells // BLK
    rank = raw_cell.shape[0]

    def fetch(n):
        rows = pl.ds(n * BLK, BLK)
        return pltpu.make_async_copy(tensor.at[rows], t_buf.at[rows], t_sem.at[n])

    for n in range(chunks):
        fetch(n).start()
    mask[...] = expand_rows(present[...])
    total = got[0]
    for d in range(1, got.shape[0]):
        total = total + got[d]
    gram = unpack(total[2 * rank :])
    col, row = scales(gram, cells_all)
    unit = gram / (col * row)
    unit_out[...] = unit
    inv = inverse(unit * gram_feat[...])
    for h in range(2):
        half = total[h * rank : (h + 1) * rank] / col
        raw_cyc[:, h * LANES : (h + 1) * LANES] = dot(inv[:, :rank], half, ((1,), (0,)), HIGHEST)
    raw_cyc_out[...] = raw_cyc[...]
    cell_t = raw_cell[...] / col
    cell_unit[...] = cell_t

    def step(n, carry):
        acc, rolled = carry
        fetch(n).wait()
        hi, lo = split(raw_cyc[...] * mask[pl.ds(n, 1), :])
        left = jnp.concatenate([hi, lo], axis=0)
        for q in range(BLK):
            hi, lo = split(t_buf[n * BLK + q])
            wide[q] = dot(left, jnp.concatenate([hi, lo], axis=1), ((1,), (0,)))
        for q in range(BLK):
            w = wide[q, :rank, :LANES] + (wide[q, :rank, LANES:] + wide[q, rank:, :LANES])
            acc = acc + w * rolled[:, q : q + 1]
        return acc, pltpu.roll(rolled, LANES - BLK, 1)

    acc, _ = lax.fori_loop(0, chunks, step, (jnp.zeros((rank, LANES), F32), cell_t))
    pay[0:rank, :] = acc
    pay[rank:, :] = pack(wide_gram(raw_cyc[...]))


def pair_kernel(mine, other, pay):
    total = mine[...] + other[...]
    for d in range(pay.shape[0]):
        pay[d] = total


def feats_kernel(cycles_all, got, raw_cyc, unit_cell, cyc_unit, raw_out, pay):
    rank = raw_cyc.shape[0]
    total = got[0]
    for d in range(1, got.shape[0]):
        total = total + got[d]
    gram = unpack(got[0, rank:, :])
    col, row = scales(gram, cycles_all)
    inv = inverse(unit_cell[...] * (gram / (col * row)))
    raw = dot(inv[:, :rank], total[:rank] / col, ((1,), (0,)), HIGHEST)
    raw_out[...] = raw
    square = jnp.broadcast_to(jnp.sum(raw * raw, axis=1, keepdims=True), (rank, LANES))
    for d in range(pay.shape[0]):
        pay[d] = square
    cyc_unit[...] = raw_cyc[...] / col


def last_kernel(feats_all, got, raw, feat_unit):
    total = got[0]
    for d in range(1, got.shape[0]):
        total = total + got[d]
    feat_unit[...] = raw[...] / jnp.sqrt(total / feats_all + EPS)


def shape(*dims):
    return jax.ShapeDtypeStruct(dims, F32)


PARAMS = pltpu.CompilerParams(vmem_limit_bytes=VMEM_LIMIT)
ANY = pl.BlockSpec(memory_space=pl.ANY)
VMEM = pl.BlockSpec(memory_space=pltpu.VMEM)


def shards(tensor, present, cyc_factor, feat_factor):
    cells, cycles, feats = tensor.shape
    rank = cyc_factor.shape[1]
    chunks = cells // BLK
    n_cell, n_cyc, n_feat = (lax.axis_size(a) for a in ("cell", "cyc", "feat"))
    c, pay = pl.pallas_call(
        contract_kernel,
        out_shape=(shape(cells, rank, cycles), shape(n_cyc * n_feat, rank + 16, LANES)),
        in_specs=[VMEM, VMEM, VMEM, ANY],
        out_specs=(ANY, VMEM),
        scratch_shapes=[
            pltpu.VMEM((cells, cycles, feats), F32),
            pltpu.VMEM((cells, rank, cycles), F32),
            pltpu.VMEM((chunks, cycles), F32),
            pltpu.VMEM((2 * rank, 2 * feats), BF16),
            pltpu.SemaphoreType.DMA((chunks,)),
            pltpu.SemaphoreType.DMA((chunks,)),
        ],
        compiler_params=PARAMS,
        name="contract",
    )(present, cyc_factor.T, feat_factor.T, tensor)
    got = lax.all_to_all(pay, ("cyc", "feat"), 0, 0)
    raw_cell, gram_feat, pay = pl.pallas_call(
        cells_kernel,
        out_shape=(shape(rank, cells), shape(rank, LANES), shape(n_feat, 2 * rank + 8, LANES)),
        in_specs=[VMEM, ANY],
        out_specs=(VMEM, VMEM, VMEM),
        scratch_shapes=[pltpu.VMEM((cells, rank, cycles), F32), pltpu.SemaphoreType.DMA((chunks,))],
        compiler_params=PARAMS,
        name="cells",
    )(got, c)
    got = lax.all_to_all(pay, "feat", 0, 0)
    pay = pl.pallas_call(
        functools.partial(spread_kernel, 2 * rank),
        out_shape=shape(n_cell, 2 * rank + 8, LANES),
        name="spread",
    )(got)
    got = lax.all_to_all(pay, "cell", 0, 0)
    cell_unit, raw_cyc, unit_cell, pay = pl.pallas_call(
        functools.partial(cycles_kernel, float(cells * n_cell)),
        out_shape=(shape(rank, cells), shape(rank, cycles), shape(rank, LANES), shape(rank + 8, LANES)),
        in_specs=[VMEM, VMEM, VMEM, VMEM, ANY],
        out_specs=(VMEM, VMEM, VMEM, VMEM),
        scratch_shapes=[
            pltpu.VMEM((cells, cycles, feats), F32),
            pltpu.VMEM((chunks, cycles), F32),
            pltpu.VMEM((rank, cycles), F32),
            pltpu.VMEM((BLK, 2 * rank, 2 * feats), F32),
            pltpu.SemaphoreType.DMA((chunks,)),
        ],
        compiler_params=PARAMS,
        name="cycles",
    )(present, got, raw_cell, gram_feat, tensor)
    other = lax.ppermute(pay, "cyc", [(i, n_cyc - 1 - i) for i in range(n_cyc)])
    pay = pl.pallas_call(pair_kernel, out_shape=shape(n_cell, rank + 8, LANES), name="pair")(pay, other)
    got = lax.all_to_all(pay, "cell", 0, 0)
    cyc_unit, raw_feat, pay = pl.pallas_call(
        functools.partial(feats_kernel, float(cycles * n_cyc)),
        out_shape=(shape(rank, cycles), shape(rank, feats), shape(n_feat, rank, LANES)),
        name="feats",
    )(got, raw_cyc, unit_cell)
    got = lax.all_to_all(pay, "feat", 0, 0)
    feat_unit = pl.pallas_call(
        functools.partial(last_kernel, float(feats * n_feat)),
        out_shape=shape(rank, feats),
        name="last",
    )(got, raw_feat)
    return cell_unit.T, cyc_unit.T, feat_unit.T


def solution(mesh):
    placed = (P("cell", "cyc", "feat"), P("cell", "cyc"), P("cyc", None), P("feat", None))
    return jax.shard_map(
        shards,
        mesh=mesh,
        in_specs=placed,
        out_specs=(P("cell", None), P("cyc", None), P("feat", None)),
        check_vma=False,
    )
```

```python
import functools

import jax
import jax.numpy as jnp
from jax import lax
from jax.experimental import pallas as pl
from jax.experimental.pallas import tpu as pltpu
from jax.sharding import PartitionSpec as P

BLK = 16
EPS = 1e-06
HIGHEST = lax.Precision.HIGHEST
F32 = jnp.float32
BF16 = jnp.bfloat16
VMEM_LIMIT = 48 * 1024 * 1024
LANES = 128


def dot(a, b, dims, precision=None):
    return lax.dot_general(a, b, (dims, ((), ())), precision=precision, preferred_element_type=F32)


def split(x):
    hi = x.astype(BF16)
    return hi, (x - hi.astype(F32)).astype(BF16)


def lane_iota(rows, cols=LANES):
    return lax.broadcasted_iota(jnp.int32, (rows, cols), 1)


def wide_gram(rows_t):
    r, n = rows_t.shape
    padded = jnp.concatenate([rows_t, jnp.zeros((LANES - r, n), F32)], axis=0)
    return dot(rows_t, padded, ((1,), (1,)), HIGHEST)


def pack(wide):
    out = wide[0:8]
    for q in range(1, 4):
        out = out + pltpu.roll(wide[8 * q : 8 * q + 8], 32 * q, 1)
    return out


def unpack(packed):
    used = lane_iota(8) < 32
    parts = [packed if q == 0 else pltpu.roll(packed, LANES - 32 * q, 1) for q in range(4)]
    return jnp.concatenate([jnp.where(used, x, 0.0) for x in parts], axis=0)


def inverse(m, width=16):
    row_id = lax.broadcasted_iota(jnp.int32, m.shape, 0)
    col_id = lax.broadcasted_iota(jnp.int32, m.shape, 1)
    for start in range(0, m.shape[0], width):
        cols = [jnp.broadcast_to(m[:, start + k : start + k + 1], m.shape) for k in range(width)]
        for k in range(width):
            p = start + k
            col = cols[k]
            d = 1.0 / col[p : p + 1, :]
            row = jnp.where(col_id[0:1] == p, d, m[p : p + 1, :] * d)
            here = row_id == p
            m = jnp.where(here, row, jnp.where(col_id == p, 0.0, m) - col * row)
            for q in range(k + 1, width):
                f = cols[q][p : p + 1, :] * d
                cols[q] = jnp.where(here, f, cols[q] - col * f)
    return m


def scales(wide, count):
    r = wide.shape[0]
    row_id = lax.broadcasted_iota(jnp.int32, wide.shape, 0)
    col_id = lax.broadcasted_iota(jnp.int32, wide.shape, 1)
    diag = jnp.where(row_id == col_id, wide, 0.0)
    col = jnp.sqrt(jnp.sum(diag, axis=1, keepdims=True) / count + EPS)
    row = jnp.sqrt(jnp.sum(diag, axis=0, keepdims=True) / count + EPS)
    return col, row


def expand_rows(present):
    nb, mb = present.shape
    first = lax.broadcasted_iota(jnp.int32, (mb, mb * BLK), 0) * BLK
    cyc = lax.broadcasted_iota(jnp.int32, (mb, mb * BLK), 1)
    spread = jnp.where((cyc >= first) & (cyc < first + BLK), 1.0, 0.0)
    return dot(present.astype(F32), spread, ((1,), (0,)), HIGHEST)


def contract_kernel(
    present_in, cyc_in, feat_in, tensor, c_out, pay, t_buf, c_buf, present, cyc_t, feat_t, mask, lhs, t_sem, c_sem, in_sem
):
    cells = tensor.shape[0]
    chunks = cells // BLK
    rank = cyc_t.shape[0]
    small = [
        pltpu.make_async_copy(src, dst, in_sem.at[n])
        for n, (src, dst) in enumerate(((present_in, present), (cyc_in, cyc_t), (feat_in, feat_t)))
    ]

    def fetch(n):
        rows = pl.ds(n * BLK, BLK)
        return pltpu.make_async_copy(tensor.at[rows], t_buf.at[rows], t_sem.at[n])

    def flush(n):
        rows = pl.ds(n * BLK, BLK)
        return pltpu.make_async_copy(c_buf.at[rows], c_out.at[rows], c_sem.at[n])

    for copy in small:
        copy.start()
    for n in range(chunks):
        fetch(n).start()
    for copy in small:
        copy.wait()
    mask[...] = expand_rows(present[...])
    hi, lo = split(feat_t[...])
    lhs[0:rank, :] = jnp.concatenate([hi, hi], axis=1)
    lhs[rank:, :] = jnp.concatenate([lo, jnp.zeros_like(lo)], axis=1)
    gram_cyc = pack(wide_gram(cyc_t[...]))
    gram_feat = pack(wide_gram(feat_t[...]))
    lane = lane_iota(rank)

    def step(n, part):
        fetch(n).wait()
        row = mask[pl.ds(n, 1), :]
        left = lhs[...]
        for q in range(BLK):
            i = n * BLK + q
            hi, lo = split(t_buf[i])
            out = dot(left, jnp.concatenate([hi, lo], axis=1), ((1,), (1,)))
            c = out[:rank] * row + out[rank:] * row
            c_buf[i] = c
            total = jnp.sum(c * cyc_t[...], axis=1, keepdims=True)
            part = jnp.where(lane == i, total, part)
        flush(n).start()
        return part

    part = lax.fori_loop(0, chunks, step, jnp.zeros((rank, cells), F32))
    for d in range(pay.shape[0]):
        pay[d, 0:rank, :] = part
        pay[d, rank : rank + 8, :] = gram_cyc
        pay[d, rank + 8 :, :] = gram_feat
    for n in range(chunks):
        flush(n).wait()


def cells_kernel(got, c_in, raw_out, gram_feat_out, pay, c_buf, c_sem):
    cells, rank = c_in.shape[0], c_in.shape[1]
    chunks = cells // BLK

    def fetch(n):
        rows = pl.ds(n * BLK, BLK)
        return pltpu.make_async_copy(c_in.at[rows], c_buf.at[rows], c_sem.at[n])

    for n in range(chunks):
        fetch(n).start()
    part = got[0, 0:rank, :]
    for d in range(1, 8):
        part = part + got[d, 0:rank, :]
    gram_cyc = unpack(got[0, rank : rank + 8, :] + got[4, rank : rank + 8, :])
    gram_feat = got[0, rank + 8 :, :]
    for d in range(1, 4):
        gram_feat = gram_feat + got[d, rank + 8 :, :]
    gram_feat = unpack(gram_feat)
    gram_feat_out[...] = gram_feat
    inv = inverse(gram_cyc * gram_feat)
    raw = dot(inv[:, :rank], part, ((1,), (0,)), HIGHEST)
    raw_out[...] = raw
    gram = pack(wide_gram(raw))

    def step(n, carry):
        fetch(n).wait()
        total, rolled = carry
        for q in range(BLK):
            total = total + c_buf[n * BLK + q] * rolled[:, q : q + 1]
        return total, pltpu.roll(rolled, LANES - BLK, 1)

    total, _ = lax.fori_loop(0, chunks, step, (jnp.zeros((rank, c_in.shape[2]), F32), raw))
    for d in range(pay.shape[0]):
        pay[d, 0:rank, :] = total[:, :LANES]
        pay[d, rank : 2 * rank, :] = total[:, LANES:]
        pay[d, 2 * rank :, :] = gram


def spread_kernel(rows, got, pay):
    total = got[0]
    for d in range(1, got.shape[0]):
        total = total + got[d]
    for d in range(pay.shape[0]):
        pay[d, :rows, :] = total[:rows]
        pay[d, rows:, :] = got[0, rows:, :]


def cycles_kernel(
    cells_all, present, got, raw_cell, gram_feat, tensor,
    cell_unit, raw_cyc_out, unit_out, pay, t_buf, mask, raw_cyc, wide, t_sem,
):
    cells = tensor.shape[0]
    chunks = cells // BLK
    rank = raw_cell.shape[0]

    def fetch(n):
        rows = pl.ds(n * BLK, BLK)
        return pltpu.make_async_copy(tensor.at[rows], t_buf.at[rows], t_sem.at[n])

    for n in range(chunks):
        fetch(n).start()
    mask[...] = expand_rows(present[...])
    total = got[0]
    for d in range(1, got.shape[0]):
        total = total + got[d]
    gram = unpack(total[2 * rank :])
    col, row = scales(gram, cells_all)
    unit = gram / (col * row)
    unit_out[...] = unit
    inv = inverse(unit * gram_feat[...])
    for h in range(2):
        half = total[h * rank : (h + 1) * rank] / col
        raw_cyc[:, h * LANES : (h + 1) * LANES] = dot(inv[:, :rank], half, ((1,), (0,)), HIGHEST)
    raw_cyc_out[...] = raw_cyc[...]
    cell_t = raw_cell[...] / col
    cell_unit[...] = cell_t

    def step(n, carry):
        acc, rolled = carry
        fetch(n).wait()
        hi, lo = split(raw_cyc[...] * mask[pl.ds(n, 1), :])
        left = jnp.concatenate([hi, lo], axis=0)
        for q in range(BLK):
            hi, lo = split(t_buf[n * BLK + q])
            wide[q] = dot(left, jnp.concatenate([hi, lo], axis=1), ((1,), (0,)))
        for q in range(BLK):
            w = wide[q, :rank, :LANES] + (wide[q, :rank, LANES:] + wide[q, rank:, :LANES])
            acc = acc + w * rolled[:, q : q + 1]
        return acc, pltpu.roll(rolled, LANES - BLK, 1)

    acc, _ = lax.fori_loop(0, chunks, step, (jnp.zeros((rank, LANES), F32), cell_t))
    gram_cyc = pack(wide_gram(raw_cyc[...]))
    for d in range(pay.shape[0]):
        pay[d, 0:rank, :] = acc
        pay[d, rank:, :] = gram_cyc


def feats_kernel(cycles_all, got, raw_cyc, unit_cell, cyc_unit, raw_out, pay):
    rank = raw_cyc.shape[0]
    total = got[0]
    for d in range(1, got.shape[0]):
        total = total + got[d]
    gram = unpack(got[0, rank:, :] + got[1, rank:, :])
    col, row = scales(gram, cycles_all)
    inv = inverse(unit_cell[...] * (gram / (col * row)))
    raw = dot(inv[:, :rank], total[:rank] / col, ((1,), (0,)), HIGHEST)
    raw_out[...] = raw
    square = jnp.broadcast_to(jnp.sum(raw * raw, axis=1, keepdims=True), (rank, LANES))
    for d in range(pay.shape[0]):
        pay[d] = square
    cyc_unit[...] = raw_cyc[...] / col


def last_kernel(feats_all, got, raw, feat_unit):
    total = got[0]
    for d in range(1, got.shape[0]):
        total = total + got[d]
    feat_unit[...] = raw[...] / jnp.sqrt(total / feats_all + EPS)


def shape(*dims):
    return jax.ShapeDtypeStruct(dims, F32)


PARAMS = pltpu.CompilerParams(vmem_limit_bytes=VMEM_LIMIT)
SMALL = pltpu.CompilerParams(vmem_limit_bytes=8 * 1024 * 1024)
ANY = pl.BlockSpec(memory_space=pl.ANY)
VMEM = pl.BlockSpec(memory_space=pltpu.VMEM)


def shards(tensor, present, cyc_factor, feat_factor):
    cells, cycles, feats = tensor.shape
    rank = cyc_factor.shape[1]
    chunks = cells // BLK
    n_cell, n_cyc, n_feat = (lax.axis_size(a) for a in ("cell", "cyc", "feat"))
    c, pay = pl.pallas_call(
        contract_kernel,
        out_shape=(shape(cells, rank, cycles), shape(n_cyc * n_feat, rank + 16, LANES)),
        in_specs=[ANY, ANY, ANY, ANY],
        out_specs=(ANY, VMEM),
        scratch_shapes=[
            pltpu.VMEM((cells, cycles, feats), F32),
            pltpu.VMEM((cells, rank, cycles), F32),
            pltpu.VMEM(present.shape, jnp.int32),
            pltpu.VMEM((rank, cycles), F32),
            pltpu.VMEM((rank, feats), F32),
            pltpu.VMEM((chunks, cycles), F32),
            pltpu.VMEM((2 * rank, 2 * feats), BF16),
            pltpu.SemaphoreType.DMA((chunks,)),
            pltpu.SemaphoreType.DMA((chunks,)),
            pltpu.SemaphoreType.DMA((3,)),
        ],
        compiler_params=PARAMS,
        name="contract",
    )(present, cyc_factor.T, feat_factor.T, tensor)
    got = lax.all_to_all(pay, ("cyc", "feat"), 0, 0)
    raw_cell, gram_feat, pay = pl.pallas_call(
        cells_kernel,
        out_shape=(shape(rank, cells), shape(rank, LANES), shape(n_feat, 2 * rank + 8, LANES)),
        in_specs=[VMEM, ANY],
        out_specs=(VMEM, VMEM, VMEM),
        scratch_shapes=[pltpu.VMEM((cells, rank, cycles), F32), pltpu.SemaphoreType.DMA((chunks,))],
        compiler_params=PARAMS,
        name="cells",
    )(got, c)
    got = lax.all_to_all(pay, "feat", 0, 0)
    pay = pl.pallas_call(
        functools.partial(spread_kernel, 2 * rank),
        out_shape=shape(n_cell, 2 * rank + 8, LANES),
        compiler_params=SMALL,
        name="spread",
    )(got)
    got = lax.all_to_all(pay, "cell", 0, 0)
    cell_unit, raw_cyc, unit_cell, pay = pl.pallas_call(
        functools.partial(cycles_kernel, float(cells * n_cell)),
        out_shape=(shape(rank, cells), shape(rank, cycles), shape(rank, LANES), shape(n_cell * n_cyc, rank + 8, LANES)),
        in_specs=[VMEM, VMEM, VMEM, VMEM, ANY],
        out_specs=(VMEM, VMEM, VMEM, VMEM),
        scratch_shapes=[
            pltpu.VMEM((cells, cycles, feats), F32),
            pltpu.VMEM((chunks, cycles), F32),
            pltpu.VMEM((rank, cycles), F32),
            pltpu.VMEM((BLK, 2 * rank, 2 * feats), F32),
            pltpu.SemaphoreType.DMA((chunks,)),
        ],
        compiler_params=PARAMS,
        name="cycles",
    )(present, got, raw_cell, gram_feat, tensor)
    got = lax.all_to_all(pay, ("cell", "cyc"), 0, 0)
    cyc_unit, raw_feat, pay = pl.pallas_call(
        functools.partial(feats_kernel, float(cycles * n_cyc)),
        out_shape=(shape(rank, cycles), shape(rank, feats), shape(n_feat, rank, LANES)),
        compiler_params=SMALL,
        name="feats",
    )(got, raw_cyc, unit_cell)
    got = lax.all_to_all(pay, "feat", 0, 0)
    feat_unit = pl.pallas_call(
        functools.partial(last_kernel, float(feats * n_feat)),
        out_shape=shape(rank, feats),
        compiler_params=SMALL,
        name="last",
    )(got, raw_feat)
    return cell_unit.T, cyc_unit.T, feat_unit.T


def solution(mesh):
    placed = (P("cell", "cyc", "feat"), P("cell", "cyc"), P("cyc", None), P("feat", None))
    return jax.shard_map(
        shards,
        mesh=mesh,
        in_specs=placed,
        out_specs=(P("cell", None), P("cyc", None), P("feat", None)),
        check_vma=False,
    )
```

```python
import functools

import jax
import jax.numpy as jnp
from jax import lax
from jax.experimental import pallas as pl
from jax.experimental.pallas import tpu as pltpu
from jax.sharding import PartitionSpec as P

BLK = 16
EPS = 1e-06
HIGHEST = lax.Precision.HIGHEST
F32 = jnp.float32
BF16 = jnp.bfloat16
LANES = 128


def dot(a, b, dims, precision=None):
    return lax.dot_general(a, b, (dims, ((), ())), precision=precision, preferred_element_type=F32)


def split(x):
    hi = x.astype(BF16)
    return hi, (x - hi.astype(F32)).astype(BF16)


def lane_iota(rows, cols=LANES):
    return lax.broadcasted_iota(jnp.int32, (rows, cols), 1)


def wide_gram(rows_t):
    r, n = rows_t.shape
    padded = jnp.concatenate([rows_t, jnp.zeros((LANES - r, n), F32)], axis=0)
    return dot(rows_t, padded, ((1,), (1,)), HIGHEST)


def pack(wide):
    out = wide[0:8]
    for q in range(1, 4):
        out = out + pltpu.roll(wide[8 * q : 8 * q + 8], 32 * q, 1)
    return out


def unpack(packed):
    used = lane_iota(8) < 32
    parts = [packed if q == 0 else pltpu.roll(packed, LANES - 32 * q, 1) for q in range(4)]
    return jnp.concatenate([jnp.where(used, x, 0.0) for x in parts], axis=0)


def inverse(m, width=16):
    row_id = lax.broadcasted_iota(jnp.int32, m.shape, 0)
    col_id = lax.broadcasted_iota(jnp.int32, m.shape, 1)
    for start in range(0, m.shape[0], width):
        cols = [jnp.broadcast_to(m[:, start + k : start + k + 1], m.shape) for k in range(width)]
        for k in range(width):
            p = start + k
            col = cols[k]
            d = 1.0 / col[p : p + 1, :]
            row = jnp.where(col_id[0:1] == p, d, m[p : p + 1, :] * d)
            here = row_id == p
            m = jnp.where(here, row, jnp.where(col_id == p, 0.0, m) - col * row)
            for q in range(k + 1, width):
                f = cols[q][p : p + 1, :] * d
                cols[q] = jnp.where(here, f, cols[q] - col * f)
    return m


def scales(wide, count):
    r = wide.shape[0]
    row_id = lax.broadcasted_iota(jnp.int32, wide.shape, 0)
    col_id = lax.broadcasted_iota(jnp.int32, wide.shape, 1)
    diag = jnp.where(row_id == col_id, wide, 0.0)
    col = jnp.sqrt(jnp.sum(diag, axis=1, keepdims=True) / count + EPS)
    row = jnp.sqrt(jnp.sum(diag, axis=0, keepdims=True) / count + EPS)
    return col, row


def expand_rows(present):
    nb, mb = present.shape
    first = lax.broadcasted_iota(jnp.int32, (mb, mb * BLK), 0) * BLK
    cyc = lax.broadcasted_iota(jnp.int32, (mb, mb * BLK), 1)
    spread = jnp.where((cyc >= first) & (cyc < first + BLK), 1.0, 0.0)
    return dot(present.astype(F32), spread, ((1,), (0,)), HIGHEST)


def tile_groups(wide):
    wide = wide + pltpu.roll(wide, 64, 1)
    return wide + pltpu.roll(wide, 32, 1)


def block_diagonal(wide):
    return jnp.concatenate([wide if g == 0 else pltpu.roll(wide, 32 * g, 1) for g in range(4)], axis=0)


def square(rows):
    n = rows.shape[0]
    return rows if n == LANES else jnp.concatenate([rows, jnp.zeros((LANES - n, LANES), F32)], axis=0)


def contract_kernel(
    present_in, cyc_in, feat_in, tensor, c_out, t_buf, pay,
    present, cyc_t, feat_t, cyc4, mask, weights, part, t_sem, in_sem,
):
    cells, cycles, feats = tensor.shape
    rank = cyc_t.shape[0]
    half = cells // 2
    piece = 8
    ahead = 2
    pieces = cells // piece
    steps = pieces // 2
    small = [
        pltpu.make_async_copy(src, dst, in_sem.at[n])
        for n, (src, dst) in enumerate(((feat_in, feat_t), (cyc_in, cyc_t), (present_in, present)))
    ]

    def fetch(n):
        rows = pl.ds(n * piece, piece)
        return pltpu.make_async_copy(tensor.at[rows], t_buf.at[rows], t_sem.at[n])

    for copy in small:
        copy.start()
    for n in range(ahead):
        fetch(n).start()
        fetch(n + steps).start()
    for copy in small:
        copy.wait()
    hi, lo = split(jnp.concatenate([feat_t[...]] * 4, axis=0).T)
    hi, lo = hi.astype(F32), lo.astype(F32)
    group = lane_iota(feats) // rank
    for g in range(2):
        weights[2 * g * feats : (2 * g + 1) * feats, :] = jnp.where(
            group == 2 * g, hi, jnp.where(group == 2 * g + 1, lo, 0.0)
        ).astype(BF16)
        weights[(2 * g + 1) * feats : (2 * g + 2) * feats, :] = jnp.where(group == 2 * g, hi, 0.0).astype(BF16)
    cyc4[...] = jnp.concatenate([cyc_t[...]] * 4, axis=0).T
    gram_cyc = pack(wide_gram(cyc_t[...]))
    gram_feat = pack(wide_gram(feat_t[...]))
    first = lane_iota(1) < LANES // 2

    def step(n, carry):
        @pl.when(n + ahead < steps)
        def _():
            fetch(n + ahead).start()
            fetch(n + ahead + steps).start()

        @pl.when(n % (BLK // piece) == 0)
        def _():
            one = n // (BLK // piece)
            two = one + half // BLK
            for b in range(cycles // BLK):
                row = jnp.where(first, present[one, b].astype(F32), present[two, b].astype(F32))
                mask[b * BLK : (b + 1) * BLK, :] = jnp.broadcast_to(row, (BLK, LANES))

        fetch(n).wait()
        fetch(n + steps).wait()
        for q in range(piece):
            p = n * piece + q
            pair = [*split(t_buf[p]), *split(t_buf[p + half])]
            c = dot(jnp.concatenate(pair, axis=1), weights[...], ((1,), (0,))) * mask[...]
            c_out[p] = c
            part[pl.ds(p, 1), :] = jnp.sum(c * cyc4[...], axis=0, keepdims=True)
        return carry

    lax.fori_loop(0, steps, step, 0, unroll=2)
    total = part[...] + pltpu.roll(part[...], LANES - rank, 1)
    total = jnp.where((lane_iota(half) // rank) % 2 == 0, total, 0.0)
    total = total[:rank] + pltpu.roll(total[rank:], rank, 1)
    for d in range(pay.shape[0]):
        pay[d, 0:rank, :] = total
        pay[d, rank : rank + 8, :] = gram_cyc
        pay[d, rank + 8 :, :] = gram_feat


def cells_kernel(got, c_in, raw_out, gram_feat_out, pay, pairs):
    half, cycles = c_in.shape[0], c_in.shape[1]
    rank = raw_out.shape[0]
    part = got[0, 0:rank, :]
    for d in range(1, 8):
        part = part + got[d, 0:rank, :]
    gram_cyc = unpack(got[0, rank : rank + 8, :] + got[4, rank : rank + 8, :])
    gram_feat = got[0, rank + 8 :, :]
    for d in range(1, 4):
        gram_feat = gram_feat + got[d, rank + 8 :, :]
    gram_feat = unpack(gram_feat)
    gram_feat_out[...] = gram_feat
    inv = inverse(gram_cyc * gram_feat)
    raw = dot(part, block_diagonal(inv), ((1,), (0,)), HIGHEST)
    raw_out[...] = raw
    even = (lane_iota(rank) // rank) % 2 == 0
    one, two = jnp.where(even, raw, 0.0), jnp.where(even, 0.0, raw)
    pairs[0:rank, :] = one + pltpu.roll(one, rank, 1)
    pairs[rank:, :] = two + pltpu.roll(two, LANES - rank, 1)
    full = dot(raw, raw, ((0,), (0,)), HIGHEST)
    gram = full[:rank]
    for g in range(1, 4):
        gram = gram + pltpu.roll(full[g * rank : (g + 1) * rank], LANES - g * rank, 1)
    gram = pack(jnp.where(lane_iota(rank) < rank, gram, 0.0))
    rows = cycles // 4
    group = lane_iota(rows) // rank
    packed = jnp.zeros((rows, LANES), F32)
    for g in range(4):

        def step(n, acc, g=g):
            for q in range(16):
                p = n * 16 + q
                acc = acc + c_in[p, g * rows : (g + 1) * rows, :] * pairs[pl.ds(p, 1), :]
            return acc

        acc = lax.fori_loop(0, half // 16, step, jnp.zeros((rows, LANES), F32))
        acc = acc + pltpu.roll(acc, 64, 1)
        acc = acc + pltpu.roll(acc, 32, 1)
        packed = jnp.where(group == g, acc, packed)
    for d in range(pay.shape[0]):
        pay[d, 0:rows, :] = packed
        pay[d, rows:, :] = gram


def spread_kernel(rows, got, pay):
    total = got[0]
    for d in range(1, got.shape[0]):
        total = total + got[d]
    for d in range(pay.shape[0]):
        pay[d, :rows, :] = total[:rows]
        pay[d, rows:, :] = got[0, rows:, :]


def cycles_kernel(
    cells_all, present, got, raw_cell, gram_feat, tensor,
    cell_unit, raw_cyc_out, unit_out, pay, mask, raw_cyc, wide,
):
    cells = tensor.shape[0]
    chunks = cells // BLK
    rank = raw_cell.shape[0]
    mask[...] = expand_rows(present[...])
    total = got[0]
    for d in range(1, got.shape[0]):
        total = total + got[d]
    gram = unpack(total[2 * rank :])
    col, row = scales(gram, cells_all)
    unit = gram / (col * row)
    unit_out[...] = unit
    inv = inverse(unit * gram_feat[...])
    scale = tile_groups(jnp.where(lane_iota(1) < rank, row, 0.0))
    raw = square(dot(total[: 2 * rank] / scale, block_diagonal(inv), ((1,), (0,)), HIGHEST)).T
    for h in range(2):
        raw_cyc[:, h * LANES : (h + 1) * LANES] = raw[2 * h * rank : (2 * h + 1) * rank] + pltpu.roll(
            raw[(2 * h + 1) * rank : (2 * h + 2) * rank], LANES // 2, 1
        )
    raw_cyc_out[...] = raw_cyc[...]
    unit_cell = square(raw_cell[...] / scale).T
    cell_t = unit_cell[:rank]
    for g in range(1, 4):
        cell_t = cell_t + pltpu.roll(unit_cell[g * rank : (g + 1) * rank], g * rank, 1)
    cell_unit[...] = cell_t

    def step(n, carry):
        acc, rolled = carry
        hi, lo = split(raw_cyc[...] * mask[pl.ds(n, 1), :])
        left = jnp.concatenate([hi, lo], axis=0)
        for q in range(BLK):
            hi, lo = split(tensor[n * BLK + q])
            wide[q] = dot(left, jnp.concatenate([hi, lo], axis=1), ((1,), (0,)))
        for q in range(BLK):
            w = wide[q, :rank, :LANES] + (wide[q, :rank, LANES:] + wide[q, rank:, :LANES])
            acc = acc + w * rolled[:, q : q + 1]
        return acc, pltpu.roll(rolled, LANES - BLK, 1)

    acc, _ = lax.fori_loop(0, chunks, step, (jnp.zeros((rank, LANES), F32), cell_t))
    gram_cyc = pack(wide_gram(raw_cyc[...]))
    for d in range(pay.shape[0]):
        pay[d, 0:rank, :] = acc
        pay[d, rank:, :] = gram_cyc


def feats_kernel(cycles_all, got, raw_cyc, unit_cell, cyc_unit, raw_out, pay):
    rank = raw_cyc.shape[0]
    total = got[0]
    for d in range(1, got.shape[0]):
        total = total + got[d]
    gram = unpack(got[0, rank:, :] + got[1, rank:, :])
    col, row = scales(gram, cycles_all)
    inv = inverse(unit_cell[...] * (gram / (col * row)))
    raw = dot(inv[:, :rank], total[:rank] / col, ((1,), (0,)), HIGHEST)
    raw_out[...] = raw
    square = jnp.broadcast_to(jnp.sum(raw * raw, axis=1, keepdims=True), (rank, LANES))
    for d in range(pay.shape[0]):
        pay[d] = square
    cyc_unit[...] = raw_cyc[...] / col


def last_kernel(feats_all, got, raw, feat_unit):
    total = got[0]
    for d in range(1, got.shape[0]):
        total = total + got[d]
    feat_unit[...] = raw[...] / jnp.sqrt(total / feats_all + EPS)


def shape(*dims):
    return jax.ShapeDtypeStruct(dims, F32)


SMALL = pltpu.CompilerParams(vmem_limit_bytes=8 * 1024 * 1024)
ANY = pl.BlockSpec(memory_space=pl.ANY)
VMEM = pl.BlockSpec(memory_space=pltpu.VMEM)


def shards(tensor, present, cyc_factor, feat_factor):
    cells, cycles, feats = tensor.shape
    rank = cyc_factor.shape[1]
    chunks = cells // BLK
    n_cell, n_cyc, n_feat = (lax.axis_size(a) for a in ("cell", "cyc", "feat"))
    far = [pltpu.with_memory_space_constraint(x, pltpu.HBM) for x in (present, cyc_factor.T, feat_factor.T, tensor)]
    c, kept, pay = pl.pallas_call(
        contract_kernel,
        out_shape=(
            pltpu.VMEM((cells // 2, cycles, LANES), F32),
            pltpu.VMEM((cells, cycles, feats), F32),
            shape(n_cyc * n_feat, rank + 16, LANES),
        ),
        in_specs=[ANY, ANY, ANY, ANY],
        out_specs=(VMEM, VMEM, VMEM),
        scratch_shapes=[
            pltpu.SMEM(present.shape, jnp.int32),
            pltpu.VMEM((rank, cycles), F32),
            pltpu.VMEM((rank, feats), F32),
            pltpu.VMEM((cycles, LANES), F32),
            pltpu.VMEM((cycles, LANES), F32),
            pltpu.VMEM((4 * feats, LANES), BF16),
            pltpu.VMEM((cells // 2, LANES), F32),
            pltpu.SemaphoreType.DMA((cells // 8,)),
            pltpu.SemaphoreType.DMA((3,)),
        ],
        compiler_params=SMALL,
        name="contract",
    )(*far)
    got = lax.all_to_all(pay, ("cyc", "feat"), 0, 0)
    raw_cell, gram_feat, pay = pl.pallas_call(
        cells_kernel,
        out_shape=(shape(rank, LANES), shape(rank, LANES), shape(n_feat, 2 * rank + 8, LANES)),
        in_specs=[VMEM, VMEM],
        out_specs=(VMEM, VMEM, VMEM),
        scratch_shapes=[pltpu.VMEM((cells // 2, LANES), F32)],
        compiler_params=SMALL,
        name="cells",
    )(got, c)
    got = lax.all_to_all(pay, "feat", 0, 0)
    pay = pl.pallas_call(
        functools.partial(spread_kernel, 2 * rank),
        out_shape=shape(n_cell, 2 * rank + 8, LANES),
        compiler_params=SMALL,
        name="spread",
    )(got)
    got = lax.all_to_all(pay, "cell", 0, 0)
    cell_unit, raw_cyc, unit_cell, pay = pl.pallas_call(
        functools.partial(cycles_kernel, float(cells * n_cell)),
        out_shape=(shape(rank, cells), shape(rank, cycles), shape(rank, LANES), shape(n_cell * n_cyc, rank + 8, LANES)),
        in_specs=[VMEM, VMEM, VMEM, VMEM, VMEM],
        out_specs=(VMEM, VMEM, VMEM, VMEM),
        scratch_shapes=[
            pltpu.VMEM((chunks, cycles), F32),
            pltpu.VMEM((rank, cycles), F32),
            pltpu.VMEM((BLK, 2 * rank, 2 * feats), F32),
        ],
        compiler_params=SMALL,
        name="cycles",
    )(present, got, raw_cell, gram_feat, kept)
    got = lax.all_to_all(pay, ("cell", "cyc"), 0, 0)
    cyc_unit, raw_feat, pay = pl.pallas_call(
        functools.partial(feats_kernel, float(cycles * n_cyc)),
        out_shape=(shape(rank, cycles), shape(rank, feats), shape(n_feat, rank, LANES)),
        compiler_params=SMALL,
        name="feats",
    )(got, raw_cyc, unit_cell)
    got = lax.all_to_all(pay, "feat", 0, 0)
    feat_unit = pl.pallas_call(
        functools.partial(last_kernel, float(feats * n_feat)),
        out_shape=shape(rank, feats),
        compiler_params=SMALL,
        name="last",
    )(got, raw_feat)
    return cell_unit.T, cyc_unit.T, feat_unit.T


def solution(mesh):
    placed = (P("cell", "cyc", "feat"), P("cell", "cyc"), P("cyc", None), P("feat", None))
    return jax.shard_map(
        shards,
        mesh=mesh,
        in_specs=placed,
        out_specs=(P("cell", None), P("cyc", None), P("feat", None)),
        check_vma=False,
    )
```

```python
import functools

import jax
import jax.numpy as jnp
from jax import lax
from jax.experimental import pallas as pl
from jax.experimental.pallas import tpu as pltpu
from jax.sharding import PartitionSpec as P

BLK = 16
EPS = 1e-06
HIGHEST = lax.Precision.HIGHEST
F32 = jnp.float32
BF16 = jnp.bfloat16
LANES = 128


def dot(a, b, dims, precision=None):
    return lax.dot_general(a, b, (dims, ((), ())), precision=precision, preferred_element_type=F32)


def split(x):
    hi = x.astype(BF16)
    return hi, (x - hi.astype(F32)).astype(BF16)


def lane_iota(rows, cols=LANES):
    return lax.broadcasted_iota(jnp.int32, (rows, cols), 1)


def wide_gram(rows_t):
    r, n = rows_t.shape
    padded = jnp.concatenate([rows_t, jnp.zeros((LANES - r, n), F32)], axis=0)
    return dot(rows_t, padded, ((1,), (1,)), HIGHEST)


def pack(wide):
    out = wide[0:8]
    for q in range(1, 4):
        out = out + pltpu.roll(wide[8 * q : 8 * q + 8], 32 * q, 1)
    return out


def unpack(packed):
    used = lane_iota(8) < 32
    parts = [packed if q == 0 else pltpu.roll(packed, LANES - 32 * q, 1) for q in range(4)]
    return jnp.concatenate([jnp.where(used, x, 0.0) for x in parts], axis=0)


def inverse(m, width=16):
    row_id = lax.broadcasted_iota(jnp.int32, m.shape, 0)
    col_id = lax.broadcasted_iota(jnp.int32, m.shape, 1)
    for start in range(0, m.shape[0], width):
        cols = [jnp.broadcast_to(m[:, start + k : start + k + 1], m.shape) for k in range(width)]
        for k in range(width):
            p = start + k
            col = cols[k]
            d = 1.0 / col[p : p + 1, :]
            row = jnp.where(col_id[0:1] == p, d, m[p : p + 1, :] * d)
            here = row_id == p
            m = jnp.where(here, row, jnp.where(col_id == p, 0.0, m) - col * row)
            for q in range(k + 1, width):
                f = cols[q][p : p + 1, :] * d
                cols[q] = jnp.where(here, f, cols[q] - col * f)
    return m


def scales(wide, count):
    r = wide.shape[0]
    row_id = lax.broadcasted_iota(jnp.int32, wide.shape, 0)
    col_id = lax.broadcasted_iota(jnp.int32, wide.shape, 1)
    diag = jnp.where(row_id == col_id, wide, 0.0)
    col = jnp.sqrt(jnp.sum(diag, axis=1, keepdims=True) / count + EPS)
    row = jnp.sqrt(jnp.sum(diag, axis=0, keepdims=True) / count + EPS)
    return col, row


def expand_rows(present):
    nb, mb = present.shape
    first = lax.broadcasted_iota(jnp.int32, (mb, mb * BLK), 0) * BLK
    cyc = lax.broadcasted_iota(jnp.int32, (mb, mb * BLK), 1)
    spread = jnp.where((cyc >= first) & (cyc < first + BLK), 1.0, 0.0)
    return dot(present.astype(F32), spread, ((1,), (0,)), HIGHEST)


def tile_groups(wide):
    wide = wide + pltpu.roll(wide, 64, 1)
    return wide + pltpu.roll(wide, 32, 1)


def block_diagonal(wide):
    return jnp.concatenate([wide if g == 0 else pltpu.roll(wide, 32 * g, 1) for g in range(4)], axis=0)


def square(rows):
    n = rows.shape[0]
    return rows if n == LANES else jnp.concatenate([rows, jnp.zeros((LANES - n, LANES), F32)], axis=0)


def contract_kernel(
    present_in, cyc_in, feat_in, tensor, c_out, t_buf, pay,
    present, cyc_t, feat_t, cyc4, mask, weights, part, t_sem, in_sem,
):
    cells, cycles, feats = tensor.shape
    rank = cyc_t.shape[0]
    half = cells // 2
    sizes = (8,) * (half // 8)
    starts = [sum(sizes[:n]) for n in range(len(sizes))]
    ahead = 2
    small = [
        pltpu.make_async_copy(src, dst, in_sem.at[n])
        for n, (src, dst) in enumerate(((feat_in, feat_t), (cyc_in, cyc_t), (present_in, present)))
    ]

    def fetch(n):
        both = []
        for h in range(2):
            rows = pl.ds(starts[n] + h * half, sizes[n])
            both.append(pltpu.make_async_copy(tensor.at[rows], t_buf.at[rows], t_sem.at[2 * n + h]))
        return both

    for copy in small:
        copy.start()
    for n in range(ahead):
        for copy in fetch(n):
            copy.start()
    for copy in small:
        copy.wait()
    hi, lo = split(jnp.concatenate([feat_t[...]] * 4, axis=0).T)
    hi, lo = hi.astype(F32), lo.astype(F32)
    group = lane_iota(feats) // rank
    for g in range(2):
        weights[2 * g * feats : (2 * g + 1) * feats, :] = jnp.where(
            group == 2 * g, hi, jnp.where(group == 2 * g + 1, lo, 0.0)
        ).astype(BF16)
        weights[(2 * g + 1) * feats : (2 * g + 2) * feats, :] = jnp.where(group == 2 * g, hi, 0.0).astype(BF16)
    cyc4[...] = jnp.concatenate([cyc_t[...]] * 4, axis=0).T
    gram_cyc = pack(wide_gram(cyc_t[...]))
    gram_feat = pack(wide_gram(feat_t[...]))
    first = lane_iota(1) < LANES // 2

    for n in range(len(sizes)):
        if n + ahead < len(sizes):
            for copy in fetch(n + ahead):
                copy.start()
        if starts[n] % BLK == 0:
            one = starts[n] // BLK
            two = one + half // BLK
            for b in range(cycles // BLK):
                row = jnp.where(first, present[one, b].astype(F32), present[two, b].astype(F32))
                mask[b * BLK : (b + 1) * BLK, :] = jnp.broadcast_to(row, (BLK, LANES))
        for copy in fetch(n):
            copy.wait()
        for p in range(starts[n], starts[n] + sizes[n]):
            pair = [*split(t_buf[p]), *split(t_buf[p + half])]
            c = dot(jnp.concatenate(pair, axis=1), weights[...], ((1,), (0,))) * mask[...]
            c_out[p] = c
            part[p : p + 1, :] = jnp.sum(c * cyc4[...], axis=0, keepdims=True)

    total = part[...] + pltpu.roll(part[...], LANES - rank, 1)
    total = jnp.where((lane_iota(half) // rank) % 2 == 0, total, 0.0)
    total = total[:rank] + pltpu.roll(total[rank:], rank, 1)
    for d in range(pay.shape[0]):
        pay[d, 0:rank, :] = total
        pay[d, rank : rank + 8, :] = gram_cyc
        pay[d, rank + 8 :, :] = gram_feat


def cells_kernel(got, c_in, raw_out, gram_feat_out, pay, pairs):
    half, cycles = c_in.shape[0], c_in.shape[1]
    rank = raw_out.shape[0]
    part = got[0, 0:rank, :]
    for d in range(1, 8):
        part = part + got[d, 0:rank, :]
    gram_cyc = unpack(got[0, rank : rank + 8, :] + got[4, rank : rank + 8, :])
    gram_feat = got[0, rank + 8 :, :]
    for d in range(1, 4):
        gram_feat = gram_feat + got[d, rank + 8 :, :]
    gram_feat = unpack(gram_feat)
    gram_feat_out[...] = gram_feat
    inv = inverse(gram_cyc * gram_feat)
    raw = dot(part, block_diagonal(inv), ((1,), (0,)), HIGHEST)
    raw_out[...] = raw
    even = (lane_iota(rank) // rank) % 2 == 0
    one, two = jnp.where(even, raw, 0.0), jnp.where(even, 0.0, raw)
    pairs[0:rank, :] = one + pltpu.roll(one, rank, 1)
    pairs[rank:, :] = two + pltpu.roll(two, LANES - rank, 1)
    full = dot(raw, raw, ((0,), (0,)), HIGHEST)
    gram = full[:rank]
    for g in range(1, 4):
        gram = gram + pltpu.roll(full[g * rank : (g + 1) * rank], LANES - g * rank, 1)
    gram = pack(jnp.where(lane_iota(rank) < rank, gram, 0.0))
    rows = cycles // 4
    group = lane_iota(rows) // rank
    packed = jnp.zeros((rows, LANES), F32)
    for g in range(4):

        def step(n, acc, g=g):
            for q in range(16):
                p = n * 16 + q
                acc = acc + c_in[p, g * rows : (g + 1) * rows, :] * pairs[pl.ds(p, 1), :]
            return acc

        acc = lax.fori_loop(0, half // 16, step, jnp.zeros((rows, LANES), F32))
        acc = acc + pltpu.roll(acc, 64, 1)
        acc = acc + pltpu.roll(acc, 32, 1)
        packed = jnp.where(group == g, acc, packed)
    for d in range(pay.shape[0]):
        pay[d, 0:rows, :] = packed
        pay[d, rows:, :] = gram


def spread_kernel(rows, got, pay):
    total = got[0]
    for d in range(1, got.shape[0]):
        total = total + got[d]
    for d in range(pay.shape[0]):
        pay[d, :rows, :] = total[:rows]
        pay[d, rows:, :] = got[0, rows:, :]


def cycles_kernel(
    cells_all, present, got, raw_cell, gram_feat, tensor,
    cell_unit, raw_cyc_out, unit_out, pay, mask, raw_cyc, cell_buf, wide, sem,
):
    cells = tensor.shape[0]
    chunks = cells // BLK
    rank = raw_cell.shape[0]
    mask[...] = expand_rows(present[...])
    total = got[0]
    for d in range(1, got.shape[0]):
        total = total + got[d]
    gram = unpack(total[2 * rank :])
    col, row = scales(gram, cells_all)
    unit = gram / (col * row)
    unit_out[...] = unit
    inv = inverse(unit * gram_feat[...])
    scale = tile_groups(jnp.where(lane_iota(1) < rank, row, 0.0))
    raw = square(dot(total[: 2 * rank] / scale, block_diagonal(inv), ((1,), (0,)), HIGHEST)).T
    for h in range(2):
        raw_cyc[:, h * LANES : (h + 1) * LANES] = raw[2 * h * rank : (2 * h + 1) * rank] + pltpu.roll(
            raw[(2 * h + 1) * rank : (2 * h + 2) * rank], LANES // 2, 1
        )
    raw_cyc_out[...] = raw_cyc[...]
    unit_cell = square(raw_cell[...] / scale).T
    cell_t = unit_cell[:rank]
    for g in range(1, 4):
        cell_t = cell_t + pltpu.roll(unit_cell[g * rank : (g + 1) * rank], g * rank, 1)
    cell_buf[...] = cell_t
    leave = pltpu.make_async_copy(cell_buf, cell_unit, sem.at[0])
    leave.start()

    def step(n, carry):
        acc, rolled = carry
        hi, lo = split(raw_cyc[...] * mask[pl.ds(n, 1), :])
        left = jnp.concatenate([hi, lo], axis=0)
        for q in range(BLK):
            hi, lo = split(tensor[n * BLK + q])
            wide[q] = dot(left, jnp.concatenate([hi, lo], axis=1), ((1,), (0,)))
        for q in range(BLK):
            w = wide[q, :rank, :LANES] + (wide[q, :rank, LANES:] + wide[q, rank:, :LANES])
            acc = acc + w * rolled[:, q : q + 1]
        return acc, pltpu.roll(rolled, LANES - BLK, 1)

    acc, _ = lax.fori_loop(0, chunks, step, (jnp.zeros((rank, LANES), F32), cell_t))
    pay[0:rank, :] = acc
    pay[rank:, :] = pack(wide_gram(raw_cyc[...]))
    leave.wait()


def pair_kernel(mine, other, pay):
    for d in range(pay.shape[0]):
        pay[d] = mine[...] + other[...]


def feats_kernel(cycles_all, got, raw_cyc, unit_cell, cyc_unit, raw_out, pay, cyc_buf, sem):
    rank = raw_cyc.shape[0]
    total = got[0]
    for d in range(1, got.shape[0]):
        total = total + got[d]
    gram = unpack(got[0, rank:, :])
    col, row = scales(gram, cycles_all)
    cyc_buf[...] = raw_cyc[...] / col
    leave = pltpu.make_async_copy(cyc_buf, cyc_unit, sem.at[0])
    leave.start()
    inv = inverse(unit_cell[...] * (gram / (col * row)))
    raw = dot(inv[:, :rank], total[:rank] / col, ((1,), (0,)), HIGHEST)
    raw_out[...] = raw
    square = jnp.broadcast_to(jnp.sum(raw * raw, axis=1, keepdims=True), (rank, LANES))
    for d in range(pay.shape[0]):
        pay[d] = square
    leave.wait()


def last_kernel(feats_all, got, raw, feat_unit):
    total = got[0]
    for d in range(1, got.shape[0]):
        total = total + got[d]
    feat_unit[...] = raw[...] / jnp.sqrt(total / feats_all + EPS)


def shape(*dims):
    return jax.ShapeDtypeStruct(dims, F32)


SMALL = pltpu.CompilerParams(vmem_limit_bytes=8 * 1024 * 1024)
ANY = pl.BlockSpec(memory_space=pl.ANY)
VMEM = pl.BlockSpec(memory_space=pltpu.VMEM)


def shards(tensor, present, cyc_factor, feat_factor):
    cells, cycles, feats = tensor.shape
    rank = cyc_factor.shape[1]
    chunks = cells // BLK
    n_cell, n_cyc, n_feat = (lax.axis_size(a) for a in ("cell", "cyc", "feat"))
    far = [pltpu.with_memory_space_constraint(x, pltpu.HBM) for x in (present, cyc_factor.T, feat_factor.T, tensor)]
    c, kept, pay = pl.pallas_call(
        contract_kernel,
        out_shape=(
            pltpu.VMEM((cells // 2, cycles, LANES), F32),
            pltpu.VMEM((cells, cycles, feats), F32),
            shape(n_cyc * n_feat, rank + 16, LANES),
        ),
        in_specs=[ANY, ANY, ANY, ANY],
        out_specs=(VMEM, VMEM, VMEM),
        scratch_shapes=[
            pltpu.SMEM(present.shape, jnp.int32),
            pltpu.VMEM((rank, cycles), F32),
            pltpu.VMEM((rank, feats), F32),
            pltpu.VMEM((cycles, LANES), F32),
            pltpu.VMEM((cycles, LANES), F32),
            pltpu.VMEM((4 * feats, LANES), BF16),
            pltpu.VMEM((cells // 2, LANES), F32),
            pltpu.SemaphoreType.DMA((cells // 4,)),
            pltpu.SemaphoreType.DMA((3,)),
        ],
        compiler_params=SMALL,
        name="contract",
    )(*far)
    got = lax.all_to_all(pay, ("cyc", "feat"), 0, 0)
    raw_cell, gram_feat, pay = pl.pallas_call(
        cells_kernel,
        out_shape=(shape(rank, LANES), shape(rank, LANES), shape(n_feat, 2 * rank + 8, LANES)),
        in_specs=[VMEM, VMEM],
        out_specs=(VMEM, VMEM, VMEM),
        scratch_shapes=[pltpu.VMEM((cells // 2, LANES), F32)],
        compiler_params=SMALL,
        name="cells",
    )(got, c)
    got = lax.all_to_all(pay, "feat", 0, 0)
    pay = pl.pallas_call(
        functools.partial(spread_kernel, 2 * rank),
        out_shape=shape(n_cell, 2 * rank + 8, LANES),
        compiler_params=SMALL,
        name="spread",
    )(got)
    got = lax.all_to_all(pay, "cell", 0, 0)
    cell_unit, raw_cyc, unit_cell, pay = pl.pallas_call(
        functools.partial(cycles_kernel, float(cells * n_cell)),
        out_shape=(pltpu.HBM((rank, cells), F32), shape(rank, cycles), shape(rank, LANES), shape(rank + 8, LANES)),
        in_specs=[VMEM, VMEM, VMEM, VMEM, VMEM],
        out_specs=(ANY, VMEM, VMEM, VMEM),
        scratch_shapes=[
            pltpu.VMEM((chunks, cycles), F32),
            pltpu.VMEM((rank, cycles), F32),
            pltpu.VMEM((rank, cells), F32),
            pltpu.VMEM((BLK, 2 * rank, 2 * feats), F32),
            pltpu.SemaphoreType.DMA((1,)),
        ],
        compiler_params=SMALL,
        name="cycles",
    )(present, got, raw_cell, gram_feat, kept)
    other = lax.ppermute(pay, "cyc", [(i, n_cyc - 1 - i) for i in range(n_cyc)])
    pay = pl.pallas_call(
        pair_kernel,
        out_shape=shape(n_cell, rank + 8, LANES),
        compiler_params=SMALL,
        name="pair",
    )(pay, other)
    got = lax.all_to_all(pay, "cell", 0, 0)
    cyc_unit, raw_feat, pay = pl.pallas_call(
        functools.partial(feats_kernel, float(cycles * n_cyc)),
        out_shape=(pltpu.HBM((rank, cycles), F32), shape(rank, feats), shape(n_feat, rank, LANES)),
        in_specs=[VMEM, VMEM, VMEM],
        out_specs=(ANY, VMEM, VMEM),
        scratch_shapes=[pltpu.VMEM((rank, cycles), F32), pltpu.SemaphoreType.DMA((1,))],
        compiler_params=SMALL,
        name="feats",
    )(got, raw_cyc, unit_cell)
    got = lax.all_to_all(pay, "feat", 0, 0)
    feat_unit = pl.pallas_call(
        functools.partial(last_kernel, float(feats * n_feat)),
        out_shape=shape(rank, feats),
        compiler_params=SMALL,
        name="last",
    )(got, raw_feat)
    return cell_unit.T, cyc_unit.T, feat_unit.T


def solution(mesh):
    placed = (P("cell", "cyc", "feat"), P("cell", "cyc"), P("cyc", None), P("feat", None))
    return jax.shard_map(
        shards,
        mesh=mesh,
        in_specs=placed,
        out_specs=(P("cell", None), P("cyc", None), P("feat", None)),
        check_vma=False,
    )
```

```python
import functools

import jax
import jax.numpy as jnp
from jax import lax
from jax.experimental import pallas as pl
from jax.experimental.pallas import tpu as pltpu
from jax.sharding import PartitionSpec as P

BLK = 16
EPS = 1e-06
HIGHEST = lax.Precision.HIGHEST
F32 = jnp.float32
BF16 = jnp.bfloat16
LANES = 128


def dot(a, b, dims, precision=None):
    return lax.dot_general(a, b, (dims, ((), ())), precision=precision, preferred_element_type=F32)


def split(x):
    hi = x.astype(BF16)
    return hi, (x - hi.astype(F32)).astype(BF16)


def lane_iota(rows, cols=LANES):
    return lax.broadcasted_iota(jnp.int32, (rows, cols), 1)


def wide_gram(rows_t):
    r, n = rows_t.shape
    padded = jnp.concatenate([rows_t, jnp.zeros((LANES - r, n), F32)], axis=0)
    return dot(rows_t, padded, ((1,), (1,)), HIGHEST)


def pack(wide):
    out = wide[0:8]
    for q in range(1, 4):
        out = out + pltpu.roll(wide[8 * q : 8 * q + 8], 32 * q, 1)
    return out


def unpack(packed):
    used = lane_iota(8) < 32
    parts = [packed if q == 0 else pltpu.roll(packed, LANES - 32 * q, 1) for q in range(4)]
    return jnp.concatenate([jnp.where(used, x, 0.0) for x in parts], axis=0)


def inverse(m, width=16):
    row_id = lax.broadcasted_iota(jnp.int32, m.shape, 0)
    col_id = lax.broadcasted_iota(jnp.int32, m.shape, 1)
    for start in range(0, m.shape[0], width):
        cols = [jnp.broadcast_to(m[:, start + k : start + k + 1], m.shape) for k in range(width)]
        for k in range(width):
            p = start + k
            col = cols[k]
            d = 1.0 / col[p : p + 1, :]
            row = jnp.where(col_id[0:1] == p, d, m[p : p + 1, :] * d)
            here = row_id == p
            m = jnp.where(here, row, jnp.where(col_id == p, 0.0, m) - col * row)
            for q in range(k + 1, width):
                f = cols[q][p : p + 1, :] * d
                cols[q] = jnp.where(here, f, cols[q] - col * f)
    return m


def scales(wide, count):
    r = wide.shape[0]
    row_id = lax.broadcasted_iota(jnp.int32, wide.shape, 0)
    col_id = lax.broadcasted_iota(jnp.int32, wide.shape, 1)
    diag = jnp.where(row_id == col_id, wide, 0.0)
    col = jnp.sqrt(jnp.sum(diag, axis=1, keepdims=True) / count + EPS)
    row = jnp.sqrt(jnp.sum(diag, axis=0, keepdims=True) / count + EPS)
    return col, row


def expand_rows(present):
    nb, mb = present.shape
    first = lax.broadcasted_iota(jnp.int32, (mb, mb * BLK), 0) * BLK
    cyc = lax.broadcasted_iota(jnp.int32, (mb, mb * BLK), 1)
    spread = jnp.where((cyc >= first) & (cyc < first + BLK), 1.0, 0.0)
    return dot(present.astype(F32), spread, ((1,), (0,)), HIGHEST)


def tile_groups(wide):
    wide = wide + pltpu.roll(wide, 64, 1)
    return wide + pltpu.roll(wide, 32, 1)


def block_diagonal(wide):
    return jnp.concatenate([wide if g == 0 else pltpu.roll(wide, 32 * g, 1) for g in range(4)], axis=0)


def square(rows):
    n = rows.shape[0]
    return rows if n == LANES else jnp.concatenate([rows, jnp.zeros((LANES - n, LANES), F32)], axis=0)


def contract_kernel(
    present_in, cyc_in, feat_in, tensor, c_out, t_buf, pay,
    present, cyc_t, feat_t, cyc4, mask, weights, part, t_sem, in_sem,
):
    cells, cycles, feats = tensor.shape
    rank = cyc_t.shape[0]
    half = cells // 2
    sizes = (8,) * (half // 8)
    starts = [sum(sizes[:n]) for n in range(len(sizes))]
    ahead = 2
    small = [
        pltpu.make_async_copy(src, dst, in_sem.at[n])
        for n, (src, dst) in enumerate(((feat_in, feat_t), (cyc_in, cyc_t), (present_in, present)))
    ]

    def fetch(n):
        both = []
        for h in range(2):
            rows = pl.ds(starts[n] + h * half, sizes[n])
            both.append(pltpu.make_async_copy(tensor.at[rows], t_buf.at[rows], t_sem.at[2 * n + h]))
        return both

    for copy in small:
        copy.start()
    for n in range(ahead):
        for copy in fetch(n):
            copy.start()
    for copy in small:
        copy.wait()
    hi, lo = split(jnp.concatenate([feat_t[...]] * 4, axis=0).T)
    hi, lo = hi.astype(F32), lo.astype(F32)
    group = lane_iota(feats) // rank
    for g in range(2):
        weights[2 * g * feats : (2 * g + 1) * feats, :] = jnp.where(
            group == 2 * g, hi, jnp.where(group == 2 * g + 1, lo, 0.0)
        ).astype(BF16)
        weights[(2 * g + 1) * feats : (2 * g + 2) * feats, :] = jnp.where(group == 2 * g, hi, 0.0).astype(BF16)
    cyc4[...] = jnp.concatenate([cyc_t[...]] * 4, axis=0).T
    gram_cyc = pack(wide_gram(cyc_t[...]))
    gram_feat = pack(wide_gram(feat_t[...]))
    first = lane_iota(1) < LANES // 2

    for n in range(len(sizes)):
        if n + ahead < len(sizes):
            for copy in fetch(n + ahead):
                copy.start()
        if starts[n] % BLK == 0:
            one = starts[n] // BLK
            two = one + half // BLK
            for b in range(cycles // BLK):
                row = jnp.where(first, present[one, b].astype(F32), present[two, b].astype(F32))
                mask[b * BLK : (b + 1) * BLK, :] = jnp.broadcast_to(row, (BLK, LANES))
        for copy in fetch(n):
            copy.wait()
        for p in range(starts[n], starts[n] + sizes[n]):
            pair = [*split(t_buf[p]), *split(t_buf[p + half])]
            c = dot(jnp.concatenate(pair, axis=1), weights[...], ((1,), (0,))) * mask[...]
            c_out[p] = c
            part[p : p + 1, :] = jnp.sum(c * cyc4[...], axis=0, keepdims=True)

    total = part[...] + pltpu.roll(part[...], LANES - rank, 1)
    total = jnp.where((lane_iota(half) // rank) % 2 == 0, total, 0.0)
    total = total[:rank] + pltpu.roll(total[rank:], rank, 1)
    for d in range(pay.shape[0]):
        pay[d, 0:rank, :] = total
        pay[d, rank : rank + 8, :] = gram_cyc
        pay[d, rank + 8 :, :] = gram_feat


def cells_kernel(got, c_in, raw_out, gram_feat_out, pay, pairs):
    half, cycles = c_in.shape[0], c_in.shape[1]
    rank = raw_out.shape[0]
    part = got[0, 0:rank, :]
    for d in range(1, 8):
        part = part + got[d, 0:rank, :]
    gram_cyc = unpack(got[0, rank : rank + 8, :] + got[4, rank : rank + 8, :])
    gram_feat = got[0, rank + 8 :, :]
    for d in range(1, 4):
        gram_feat = gram_feat + got[d, rank + 8 :, :]
    gram_feat = unpack(gram_feat)
    gram_feat_out[...] = gram_feat
    inv = inverse(gram_cyc * gram_feat)
    raw = dot(part, block_diagonal(inv), ((1,), (0,)), HIGHEST)
    raw_out[...] = raw
    even = (lane_iota(rank) // rank) % 2 == 0
    one, two = jnp.where(even, raw, 0.0), jnp.where(even, 0.0, raw)
    pairs[0:rank, :] = one + pltpu.roll(one, rank, 1)
    pairs[rank:, :] = two + pltpu.roll(two, LANES - rank, 1)
    full = dot(raw, raw, ((0,), (0,)), HIGHEST)
    gram = full[:rank]
    for g in range(1, 4):
        gram = gram + pltpu.roll(full[g * rank : (g + 1) * rank], LANES - g * rank, 1)
    gram = pack(jnp.where(lane_iota(rank) < rank, gram, 0.0))
    rows = cycles // 4
    group = lane_iota(rows) // rank
    packed = jnp.zeros((rows, LANES), F32)
    for g in range(4):

        def step(n, acc, g=g):
            for q in range(16):
                p = n * 16 + q
                acc = acc + c_in[p, g * rows : (g + 1) * rows, :] * pairs[pl.ds(p, 1), :]
            return acc

        acc = lax.fori_loop(0, half // 16, step, jnp.zeros((rows, LANES), F32), unroll=True)
        acc = acc + pltpu.roll(acc, 64, 1)
        acc = acc + pltpu.roll(acc, 32, 1)
        packed = jnp.where(group == g, acc, packed)
    for d in range(pay.shape[0]):
        pay[d, 0:rows, :] = packed
        pay[d, rows:, :] = gram


def spread_kernel(rows, got, pay):
    total = got[0]
    for d in range(1, got.shape[0]):
        total = total + got[d]
    for d in range(pay.shape[0]):
        pay[d, :rows, :] = total[:rows]
        pay[d, rows:, :] = got[0, rows:, :]


def cycles_kernel(
    cells_all, present, got, raw_cell, gram_feat, tensor,
    cell_unit, raw_cyc_out, unit_out, pay, mask, raw_cyc, cell_buf, wide, sem,
):
    cells = tensor.shape[0]
    chunks = cells // BLK
    rank = raw_cell.shape[0]
    mask[...] = expand_rows(present[...])
    total = got[0]
    for d in range(1, got.shape[0]):
        total = total + got[d]
    gram = unpack(total[2 * rank :])
    col, row = scales(gram, cells_all)
    unit = gram / (col * row)
    unit_out[...] = unit
    inv = inverse(unit * gram_feat[...])
    scale = tile_groups(jnp.where(lane_iota(1) < rank, row, 0.0))
    raw = square(dot(total[: 2 * rank] / scale, block_diagonal(inv), ((1,), (0,)), HIGHEST)).T
    for h in range(2):
        raw_cyc[:, h * LANES : (h + 1) * LANES] = raw[2 * h * rank : (2 * h + 1) * rank] + pltpu.roll(
            raw[(2 * h + 1) * rank : (2 * h + 2) * rank], LANES // 2, 1
        )
    raw_cyc_out[...] = raw_cyc[...]
    unit_cell = square(raw_cell[...] / scale).T
    cell_t = unit_cell[:rank]
    for g in range(1, 4):
        cell_t = cell_t + pltpu.roll(unit_cell[g * rank : (g + 1) * rank], g * rank, 1)
    cell_buf[...] = cell_t
    leave = pltpu.make_async_copy(cell_buf, cell_unit, sem.at[0])
    leave.start()

    def step(n, carry):
        acc, rolled = carry
        hi, lo = split(raw_cyc[...] * mask[pl.ds(n, 1), :])
        left = jnp.concatenate([hi, lo], axis=0)
        for q in range(BLK):
            hi, lo = split(tensor[n * BLK + q])
            wide[q] = dot(left, jnp.concatenate([hi, lo], axis=1), ((1,), (0,)))
        for q in range(BLK):
            w = wide[q, :rank, :LANES] + (wide[q, :rank, LANES:] + wide[q, rank:, :LANES])
            acc = acc + w * rolled[:, q : q + 1]
        return acc, pltpu.roll(rolled, LANES - BLK, 1)

    acc, _ = lax.fori_loop(0, chunks, step, (jnp.zeros((rank, LANES), F32), cell_t), unroll=4)
    pay[0:rank, :] = acc
    pay[rank:, :] = pack(wide_gram(raw_cyc[...]))
    leave.wait()


def pair_kernel(mine, other, pay):
    for d in range(pay.shape[0]):
        pay[d] = mine[...] + other[...]


def feats_kernel(cycles_all, got, raw_cyc, unit_cell, cyc_unit, raw_out, pay, cyc_buf, sem):
    rank = raw_cyc.shape[0]
    total = got[0]
    for d in range(1, got.shape[0]):
        total = total + got[d]
    gram = unpack(got[0, rank:, :])
    col, row = scales(gram, cycles_all)
    cyc_buf[...] = raw_cyc[...] / col
    leave = pltpu.make_async_copy(cyc_buf, cyc_unit, sem.at[0])
    leave.start()
    inv = inverse(unit_cell[...] * (gram / (col * row)))
    raw = dot(inv[:, :rank], total[:rank] / col, ((1,), (0,)), HIGHEST)
    raw_out[...] = raw
    square = jnp.broadcast_to(jnp.sum(raw * raw, axis=1, keepdims=True), (rank, LANES))
    for d in range(pay.shape[0]):
        pay[d] = square
    leave.wait()


def last_kernel(feats_all, got, raw, feat_unit):
    total = got[0]
    for d in range(1, got.shape[0]):
        total = total + got[d]
    feat_unit[...] = raw[...] / jnp.sqrt(total / feats_all + EPS)


def shape(*dims):
    return jax.ShapeDtypeStruct(dims, F32)


SMALL = pltpu.CompilerParams(vmem_limit_bytes=8 * 1024 * 1024)
ANY = pl.BlockSpec(memory_space=pl.ANY)
VMEM = pl.BlockSpec(memory_space=pltpu.VMEM)


def shards(tensor, present, cyc_factor, feat_factor):
    cells, cycles, feats = tensor.shape
    rank = cyc_factor.shape[1]
    chunks = cells // BLK
    n_cell, n_cyc, n_feat = (lax.axis_size(a) for a in ("cell", "cyc", "feat"))
    far = [pltpu.with_memory_space_constraint(x, pltpu.HBM) for x in (present, cyc_factor.T, feat_factor.T, tensor)]
    c, kept, pay = pl.pallas_call(
        contract_kernel,
        out_shape=(
            pltpu.VMEM((cells // 2, cycles, LANES), F32),
            pltpu.VMEM((cells, cycles, feats), F32),
            shape(n_cyc * n_feat, rank + 16, LANES),
        ),
        in_specs=[ANY, ANY, ANY, ANY],
        out_specs=(VMEM, VMEM, VMEM),
        scratch_shapes=[
            pltpu.SMEM(present.shape, jnp.int32),
            pltpu.VMEM((rank, cycles), F32),
            pltpu.VMEM((rank, feats), F32),
            pltpu.VMEM((cycles, LANES), F32),
            pltpu.VMEM((cycles, LANES), F32),
            pltpu.VMEM((4 * feats, LANES), BF16),
            pltpu.VMEM((cells // 2, LANES), F32),
            pltpu.SemaphoreType.DMA((cells // 4,)),
            pltpu.SemaphoreType.DMA((3,)),
        ],
        compiler_params=SMALL,
        name="contract",
    )(*far)
    got = lax.all_to_all(pay, ("cyc", "feat"), 0, 0)
    raw_cell, gram_feat, pay = pl.pallas_call(
        cells_kernel,
        out_shape=(shape(rank, LANES), shape(rank, LANES), shape(n_feat, 2 * rank + 8, LANES)),
        in_specs=[VMEM, VMEM],
        out_specs=(VMEM, VMEM, VMEM),
        scratch_shapes=[pltpu.VMEM((cells // 2, LANES), F32)],
        compiler_params=SMALL,
        name="cells",
    )(got, c)
    got = lax.all_to_all(pay, "feat", 0, 0)
    pay = pl.pallas_call(
        functools.partial(spread_kernel, 2 * rank),
        out_shape=shape(n_cell, 2 * rank + 8, LANES),
        compiler_params=SMALL,
        name="spread",
    )(got)
    got = lax.all_to_all(pay, "cell", 0, 0)
    cell_unit, raw_cyc, unit_cell, pay = pl.pallas_call(
        functools.partial(cycles_kernel, float(cells * n_cell)),
        out_shape=(pltpu.HBM((rank, cells), F32), shape(rank, cycles), shape(rank, LANES), shape(rank + 8, LANES)),
        in_specs=[VMEM, VMEM, VMEM, VMEM, VMEM],
        out_specs=(ANY, VMEM, VMEM, VMEM),
        scratch_shapes=[
            pltpu.VMEM((chunks, cycles), F32),
            pltpu.VMEM((rank, cycles), F32),
            pltpu.VMEM((rank, cells), F32),
            pltpu.VMEM((BLK, 2 * rank, 2 * feats), F32),
            pltpu.SemaphoreType.DMA((1,)),
        ],
        compiler_params=SMALL,
        name="cycles",
    )(present, got, raw_cell, gram_feat, kept)
    other = lax.ppermute(pay, "cyc", [(i, n_cyc - 1 - i) for i in range(n_cyc)])
    pay = pl.pallas_call(
        pair_kernel,
        out_shape=shape(n_cell, rank + 8, LANES),
        compiler_params=SMALL,
        name="pair",
    )(pay, other)
    got = lax.all_to_all(pay, "cell", 0, 0)
    cyc_unit, raw_feat, pay = pl.pallas_call(
        functools.partial(feats_kernel, float(cycles * n_cyc)),
        out_shape=(pltpu.HBM((rank, cycles), F32), shape(rank, feats), shape(n_feat, rank, LANES)),
        in_specs=[VMEM, VMEM, VMEM],
        out_specs=(ANY, VMEM, VMEM),
        scratch_shapes=[pltpu.VMEM((rank, cycles), F32), pltpu.SemaphoreType.DMA((1,))],
        compiler_params=SMALL,
        name="feats",
    )(got, raw_cyc, unit_cell)
    got = lax.all_to_all(pay, "feat", 0, 0)
    feat_unit = pl.pallas_call(
        functools.partial(last_kernel, float(feats * n_feat)),
        out_shape=shape(rank, feats),
        compiler_params=SMALL,
        name="last",
    )(got, raw_feat)
    return cell_unit.T, cyc_unit.T, feat_unit.T


def solution(mesh):
    placed = (P("cell", "cyc", "feat"), P("cell", "cyc"), P("cyc", None), P("feat", None))
    return jax.shard_map(
        shards,
        mesh=mesh,
        in_specs=placed,
        out_specs=(P("cell", None), P("cyc", None), P("feat", None)),
        check_vma=False,
    )
```

```python
import functools

import jax
import jax.numpy as jnp
from jax import lax
from jax.experimental import pallas as pl
from jax.experimental.pallas import tpu as pltpu
from jax.sharding import PartitionSpec as P

BLK = 16
EPS = 1e-06
HIGHEST = lax.Precision.HIGHEST
F32 = jnp.float32
BF16 = jnp.bfloat16
LANES = 128


def dot(a, b, dims, precision=None):
    return lax.dot_general(a, b, (dims, ((), ())), precision=precision, preferred_element_type=F32)


def split(x):
    hi = x.astype(BF16)
    return hi, (x - hi.astype(F32)).astype(BF16)


def lane_iota(rows, cols=LANES):
    return lax.broadcasted_iota(jnp.int32, (rows, cols), 1)


def wide_gram(rows_t):
    r, n = rows_t.shape
    padded = jnp.concatenate([rows_t, jnp.zeros((LANES - r, n), F32)], axis=0)
    return dot(rows_t, padded, ((1,), (1,)), HIGHEST)


def pack(wide):
    out = wide[0:8]
    for q in range(1, 4):
        out = out + pltpu.roll(wide[8 * q : 8 * q + 8], 32 * q, 1)
    return out


def unpack(packed):
    used = lane_iota(8) < 32
    parts = [packed if q == 0 else pltpu.roll(packed, LANES - 32 * q, 1) for q in range(4)]
    return jnp.concatenate([jnp.where(used, x, 0.0) for x in parts], axis=0)


def inverse(m, width=16):
    row_id = lax.broadcasted_iota(jnp.int32, m.shape, 0)
    col_id = lax.broadcasted_iota(jnp.int32, m.shape, 1)
    for start in range(0, m.shape[0], width):
        cols = [jnp.broadcast_to(m[:, start + k : start + k + 1], m.shape) for k in range(width)]
        for k in range(width):
            p = start + k
            col = cols[k]
            d = 1.0 / col[p : p + 1, :]
            row = jnp.where(col_id[0:1] == p, d, m[p : p + 1, :] * d)
            here = row_id == p
            m = jnp.where(here, row, jnp.where(col_id == p, 0.0, m) - col * row)
            for q in range(k + 1, width):
                f = cols[q][p : p + 1, :] * d
                cols[q] = jnp.where(here, f, cols[q] - col * f)
    return m


def scales(wide, count):
    r = wide.shape[0]
    row_id = lax.broadcasted_iota(jnp.int32, wide.shape, 0)
    col_id = lax.broadcasted_iota(jnp.int32, wide.shape, 1)
    diag = jnp.where(row_id == col_id, wide, 0.0)
    col = jnp.sqrt(jnp.sum(diag, axis=1, keepdims=True) / count + EPS)
    row = jnp.sqrt(jnp.sum(diag, axis=0, keepdims=True) / count + EPS)
    return col, row


def expand_rows(present):
    nb, mb = present.shape
    first = lax.broadcasted_iota(jnp.int32, (mb, mb * BLK), 0) * BLK
    cyc = lax.broadcasted_iota(jnp.int32, (mb, mb * BLK), 1)
    spread = jnp.where((cyc >= first) & (cyc < first + BLK), 1.0, 0.0)
    return dot(present.astype(F32), spread, ((1,), (0,)), HIGHEST)


def tile_groups(wide):
    wide = wide + pltpu.roll(wide, 64, 1)
    return wide + pltpu.roll(wide, 32, 1)


def block_diagonal(wide):
    return jnp.concatenate([wide if g == 0 else pltpu.roll(wide, 32 * g, 1) for g in range(4)], axis=0)


def square(rows):
    n = rows.shape[0]
    return rows if n == LANES else jnp.concatenate([rows, jnp.zeros((LANES - n, LANES), F32)], axis=0)


def contract_kernel(
    present_in, cyc_in, feat_in, tensor, c_out, t_buf, pay,
    present, cyc_t, feat_t, cyc4, mask, weights, part, t_sem, in_sem,
):
    cells, cycles, feats = tensor.shape
    rank = cyc_t.shape[0]
    half = cells // 2
    sizes = (8,) * (half // 8)
    starts = [sum(sizes[:n]) for n in range(len(sizes))]
    ahead = 2
    small = [
        pltpu.make_async_copy(src, dst, in_sem.at[n])
        for n, (src, dst) in enumerate(((feat_in, feat_t), (cyc_in, cyc_t), (present_in, present)))
    ]

    def fetch(n):
        both = []
        for h in range(2):
            rows = pl.ds(starts[n] + h * half, sizes[n])
            both.append(pltpu.make_async_copy(tensor.at[rows], t_buf.at[rows], t_sem.at[2 * n + h]))
        return both

    for copy in small:
        copy.start()
    for n in range(ahead):
        for copy in fetch(n):
            copy.start()
    for copy in small:
        copy.wait()
    hi, lo = split(jnp.concatenate([feat_t[...]] * 4, axis=0).T)
    hi, lo = hi.astype(F32), lo.astype(F32)
    group = lane_iota(feats) // rank
    for g in range(2):
        weights[2 * g * feats : (2 * g + 1) * feats, :] = jnp.where(
            group == 2 * g, hi, jnp.where(group == 2 * g + 1, lo, 0.0)
        ).astype(BF16)
        weights[(2 * g + 1) * feats : (2 * g + 2) * feats, :] = jnp.where(group == 2 * g, hi, 0.0).astype(BF16)
    cyc4[...] = jnp.concatenate([cyc_t[...]] * 4, axis=0).T
    gram_cyc = pack(wide_gram(cyc_t[...]))
    gram_feat = pack(wide_gram(feat_t[...]))
    first = lane_iota(1) < LANES // 2

    for n in range(len(sizes)):
        if n + ahead < len(sizes):
            for copy in fetch(n + ahead):
                copy.start()
        if starts[n] % BLK == 0:
            one = starts[n] // BLK
            two = one + half // BLK
            for b in range(cycles // BLK):
                row = jnp.where(first, present[one, b].astype(F32), present[two, b].astype(F32))
                mask[b * BLK : (b + 1) * BLK, :] = jnp.broadcast_to(row, (BLK, LANES))
        for copy in fetch(n):
            copy.wait()
        for p in range(starts[n], starts[n] + sizes[n]):
            pair = [*split(t_buf[p]), *split(t_buf[p + half])]
            c = dot(jnp.concatenate(pair, axis=1), weights[...], ((1,), (0,))) * mask[...]
            c_out[p] = c
            part[p : p + 1, :] = jnp.sum(c * cyc4[...], axis=0, keepdims=True)

    total = part[...] + pltpu.roll(part[...], LANES - rank, 1)
    total = jnp.where((lane_iota(half) // rank) % 2 == 0, total, 0.0)
    total = total[:rank] + pltpu.roll(total[rank:], rank, 1)
    for d in range(pay.shape[0]):
        pay[d, 0:rank, :] = total
        pay[d, rank : rank + 8, :] = gram_cyc
        pay[d, rank + 8 :, :] = gram_feat


def cells_kernel(got, c_in, raw_out, gram_feat_out, pay, pairs):
    half, cycles = c_in.shape[0], c_in.shape[1]
    rank = raw_out.shape[0]
    part = got[0, 0:rank, :]
    for d in range(1, 8):
        part = part + got[d, 0:rank, :]
    gram_cyc = unpack(got[0, rank : rank + 8, :] + got[4, rank : rank + 8, :])
    gram_feat = got[0, rank + 8 :, :]
    for d in range(1, 4):
        gram_feat = gram_feat + got[d, rank + 8 :, :]
    gram_feat = unpack(gram_feat)
    gram_feat_out[...] = gram_feat
    inv = inverse(gram_cyc * gram_feat)
    raw = dot(part, block_diagonal(inv), ((1,), (0,)), HIGHEST)
    raw_out[...] = raw
    even = (lane_iota(rank) // rank) % 2 == 0
    one, two = jnp.where(even, raw, 0.0), jnp.where(even, 0.0, raw)
    pairs[0:rank, :] = one + pltpu.roll(one, rank, 1)
    pairs[rank:, :] = two + pltpu.roll(two, LANES - rank, 1)
    full = dot(raw, raw, ((0,), (0,)), HIGHEST)
    gram = full[:rank]
    for g in range(1, 4):
        gram = gram + pltpu.roll(full[g * rank : (g + 1) * rank], LANES - g * rank, 1)
    gram = pack(jnp.where(lane_iota(rank) < rank, gram, 0.0))
    rows = cycles // 4
    group = lane_iota(rows) // rank
    packed = jnp.zeros((rows, LANES), F32)
    for g in range(4):

        def step(n, acc, g=g):
            for q in range(16):
                p = n * 16 + q
                acc = acc + c_in[p, g * rows : (g + 1) * rows, :] * pairs[pl.ds(p, 1), :]
            return acc

        acc = lax.fori_loop(0, half // 16, step, jnp.zeros((rows, LANES), F32), unroll=True)
        acc = acc + pltpu.roll(acc, 64, 1)
        acc = acc + pltpu.roll(acc, 32, 1)
        packed = jnp.where(group == g, acc, packed)
    for d in range(pay.shape[0]):
        pay[d, 0:rows, :] = packed
        pay[d, rows:, :] = gram


def spread_kernel(rows, got, pay):
    total = got[0]
    for d in range(1, got.shape[0]):
        total = total + got[d]
    for d in range(pay.shape[0]):
        pay[d, :rows, :] = total[:rows]
        pay[d, rows:, :] = got[0, rows:, :]


def cycles_kernel(
    cells_all, present, got, raw_cell, gram_feat, tensor,
    cell_unit, raw_cyc_out, unit_out, pay, mask, raw_cyc, cell_buf, sem,
):
    cells = tensor.shape[0]
    chunks = cells // BLK
    rank = raw_cell.shape[0]
    mask[...] = expand_rows(present[...])
    total = got[0]
    for d in range(1, got.shape[0]):
        total = total + got[d]
    gram = unpack(total[2 * rank :])
    col, row = scales(gram, cells_all)
    unit = gram / (col * row)
    unit_out[...] = unit
    inv = inverse(unit * gram_feat[...])
    scale = tile_groups(jnp.where(lane_iota(1) < rank, row, 0.0))
    raw = square(dot(total[: 2 * rank] / scale, block_diagonal(inv), ((1,), (0,)), HIGHEST)).T
    for h in range(2):
        raw_cyc[:, h * LANES : (h + 1) * LANES] = raw[2 * h * rank : (2 * h + 1) * rank] + pltpu.roll(
            raw[(2 * h + 1) * rank : (2 * h + 2) * rank], LANES // 2, 1
        )
    raw_cyc_out[...] = raw_cyc[...]
    unit_cell = square(raw_cell[...] / scale).T
    cell_t = unit_cell[:rank]
    for g in range(1, 4):
        cell_t = cell_t + pltpu.roll(unit_cell[g * rank : (g + 1) * rank], g * rank, 1)
    cell_buf[...] = cell_t
    leave = pltpu.make_async_copy(cell_buf, cell_unit, sem.at[0])
    leave.start()

    def step(n, carry):
        acc, rolled = carry
        hi, lo = split(raw_cyc[...] * mask[pl.ds(n, 1), :])
        left = jnp.concatenate([hi, lo], axis=0)
        for q in range(BLK):
            hi, lo = split(tensor[n * BLK + q])
            high = dot(left, hi, ((1,), (0,)))
            low = dot(left[:rank], lo, ((1,), (0,)))
            one = rolled[:, q : q + 1]
            acc = acc + (high[:rank] * one + (high[rank:] * one + low * one))
        return acc, pltpu.roll(rolled, LANES - BLK, 1)

    acc, _ = lax.fori_loop(0, chunks, step, (jnp.zeros((rank, LANES), F32), cell_t), unroll=4)
    pay[0:rank, :] = acc
    pay[rank:, :] = pack(wide_gram(raw_cyc[...]))
    leave.wait()


def pair_kernel(mine, other, pay):
    for d in range(pay.shape[0]):
        pay[d] = mine[...] + other[...]


def feats_kernel(cycles_all, got, raw_cyc, unit_cell, cyc_unit, raw_out, pay, cyc_buf, sem):
    rank = raw_cyc.shape[0]
    total = got[0]
    for d in range(1, got.shape[0]):
        total = total + got[d]
    gram = unpack(got[0, rank:, :])
    col, row = scales(gram, cycles_all)
    cyc_buf[...] = raw_cyc[...] / col
    leave = pltpu.make_async_copy(cyc_buf, cyc_unit, sem.at[0])
    leave.start()
    inv = inverse(unit_cell[...] * (gram / (col * row)))
    raw = dot(inv[:, :rank], total[:rank] / col, ((1,), (0,)), HIGHEST)
    raw_out[...] = raw
    square = jnp.broadcast_to(jnp.sum(raw * raw, axis=1, keepdims=True), (rank, LANES))
    for d in range(pay.shape[0]):
        pay[d] = square
    leave.wait()


def last_kernel(feats_all, got, raw, feat_unit):
    total = got[0]
    for d in range(1, got.shape[0]):
        total = total + got[d]
    feat_unit[...] = raw[...] / jnp.sqrt(total / feats_all + EPS)


def shape(*dims):
    return jax.ShapeDtypeStruct(dims, F32)


SMALL = pltpu.CompilerParams(vmem_limit_bytes=8 * 1024 * 1024)
ANY = pl.BlockSpec(memory_space=pl.ANY)
VMEM = pl.BlockSpec(memory_space=pltpu.VMEM)


def shards(tensor, present, cyc_factor, feat_factor):
    cells, cycles, feats = tensor.shape
    rank = cyc_factor.shape[1]
    chunks = cells // BLK
    n_cell, n_cyc, n_feat = (lax.axis_size(a) for a in ("cell", "cyc", "feat"))
    far = [pltpu.with_memory_space_constraint(x, pltpu.HBM) for x in (present, cyc_factor.T, feat_factor.T, tensor)]
    c, kept, pay = pl.pallas_call(
        contract_kernel,
        out_shape=(
            pltpu.VMEM((cells // 2, cycles, LANES), F32),
            pltpu.VMEM((cells, cycles, feats), F32),
            shape(n_cyc * n_feat, rank + 16, LANES),
        ),
        in_specs=[ANY, ANY, ANY, ANY],
        out_specs=(VMEM, VMEM, VMEM),
        scratch_shapes=[
            pltpu.SMEM(present.shape, jnp.int32),
            pltpu.VMEM((rank, cycles), F32),
            pltpu.VMEM((rank, feats), F32),
            pltpu.VMEM((cycles, LANES), F32),
            pltpu.VMEM((cycles, LANES), F32),
            pltpu.VMEM((4 * feats, LANES), BF16),
            pltpu.VMEM((cells // 2, LANES), F32),
            pltpu.SemaphoreType.DMA((cells // 4,)),
            pltpu.SemaphoreType.DMA((3,)),
        ],
        compiler_params=SMALL,
        name="contract",
    )(*far)
    got = lax.all_to_all(pay, ("cyc", "feat"), 0, 0)
    raw_cell, gram_feat, pay = pl.pallas_call(
        cells_kernel,
        out_shape=(shape(rank, LANES), shape(rank, LANES), shape(n_feat, 2 * rank + 8, LANES)),
        in_specs=[VMEM, VMEM],
        out_specs=(VMEM, VMEM, VMEM),
        scratch_shapes=[pltpu.VMEM((cells // 2, LANES), F32)],
        compiler_params=SMALL,
        name="cells",
    )(got, c)
    got = lax.all_to_all(pay, "feat", 0, 0)
    pay = pl.pallas_call(
        functools.partial(spread_kernel, 2 * rank),
        out_shape=shape(n_cell, 2 * rank + 8, LANES),
        compiler_params=SMALL,
        name="spread",
    )(got)
    got = lax.all_to_all(pay, "cell", 0, 0)
    cell_unit, raw_cyc, unit_cell, pay = pl.pallas_call(
        functools.partial(cycles_kernel, float(cells * n_cell)),
        out_shape=(pltpu.HBM((rank, cells), F32), shape(rank, cycles), shape(rank, LANES), shape(rank + 8, LANES)),
        in_specs=[VMEM, VMEM, VMEM, VMEM, VMEM],
        out_specs=(ANY, VMEM, VMEM, VMEM),
        scratch_shapes=[
            pltpu.VMEM((chunks, cycles), F32),
            pltpu.VMEM((rank, cycles), F32),
            pltpu.VMEM((rank, cells), F32),
            pltpu.SemaphoreType.DMA((1,)),
        ],
        compiler_params=SMALL,
        name="cycles",
    )(present, got, raw_cell, gram_feat, kept)
    other = lax.ppermute(pay, "cyc", [(i, n_cyc - 1 - i) for i in range(n_cyc)])
    pay = pl.pallas_call(
        pair_kernel,
        out_shape=shape(n_cell, rank + 8, LANES),
        compiler_params=SMALL,
        name="pair",
    )(pay, other)
    got = lax.all_to_all(pay, "cell", 0, 0)
    cyc_unit, raw_feat, pay = pl.pallas_call(
        functools.partial(feats_kernel, float(cycles * n_cyc)),
        out_shape=(pltpu.HBM((rank, cycles), F32), shape(rank, feats), shape(n_feat, rank, LANES)),
        in_specs=[VMEM, VMEM, VMEM],
        out_specs=(ANY, VMEM, VMEM),
        scratch_shapes=[pltpu.VMEM((rank, cycles), F32), pltpu.SemaphoreType.DMA((1,))],
        compiler_params=SMALL,
        name="feats",
    )(got, raw_cyc, unit_cell)
    got = lax.all_to_all(pay, "feat", 0, 0)
    feat_unit = pl.pallas_call(
        functools.partial(last_kernel, float(feats * n_feat)),
        out_shape=shape(rank, feats),
        compiler_params=SMALL,
        name="last",
    )(got, raw_feat)
    return cell_unit.T, cyc_unit.T, feat_unit.T


def solution(mesh):
    placed = (P("cell", "cyc", "feat"), P("cell", "cyc"), P("cyc", None), P("feat", None))
    return jax.shard_map(
        shards,
        mesh=mesh,
        in_specs=placed,
        out_specs=(P("cell", None), P("cyc", None), P("feat", None)),
        check_vma=False,
    )
```
